128 devices in a mesh: dp: 4 (over z_hi, core), fsdp: 32 (over z_lo, y, x).
Axes of the slice: x: 4, y: 4, z: 4 (z_hi: 2, z_lo: 2; z = z_hi * 2 + z_lo), core: 2. Of those that a mesh axis runs over, the one named last changes fastest.
Arguments:
- grad_partial: float32 [4, 160, 512, 512], P('dp', None, 'fsdp'), may hold values from -6 to 6
- params: bfloat16 [160, 512, 512], P(None, 'fsdp'), may hold values from -0.75 to 0.75
- stats_left: float32 [256, 512, 512], P(('dp', 'fsdp')), as said below
- stats_right: float32 [256, 512, 512], P(('dp', 'fsdp')), as said below
- roots_left: float32 [256, 512, 512], P(('dp', 'fsdp')), as said below
- roots_right: float32 [256, 512, 512], P(('dp', 'fsdp')), as said below
- owner: int32 [160], replicated, may hold values from 0 to 127, as said below
- refresh: int32 [160], replicated, may hold values from 0 to 1, as said below
Outputs:
- new_params: bfloat16 [160, 512, 512], P(None, 'fsdp')
- new_left: float32 [256, 512, 512], P(('dp', 'fsdp'))
- new_right: float32 [256, 512, 512], P(('dp', 'fsdp'))
The draws below stay inside these ranges and needn't reach their ends.
Inputs may be any that keep to these rules, and one draw needn't show every extreme that they name: owner[b] is the index (dp index times 32 plus fsdp index) of the device that owns block b; every device owns one or two blocks, none more than 2. refresh is 1 on exactly 20 blocks, each owned by a device that owns no other block, and 0 elsewhere; the device whose fsdp index differs from such an owner's in the lowest bit owns no block with refresh 1. `stats_left`: symmetric positive definite, smallest eigenvalue 0.05 or more. `stats_right`: symmetric positive definite, smallest eigenvalue 0.05 or more. `roots_left`: symmetric positive definite. `roots_right`: symmetric positive definite.
All inputs are finite; a program needn't handle non-finite values.
Results may differ from the reference program's by a relative error of at most 0.0051.
Values may be sent and summed in bfloat16 or wider, within the bound.
A program may use at most 128 MiB of HBM per device.

```python
import math
import jax
import jax.numpy as jnp
from jax import lax

B = 512
CAP = 2
ITERS = 6
NB = 160
NREF = 20
SLOTS = 256
N_DP = 4
N_FSDP = 32


def owner_table(key):
    devices = N_DP * N_FSDP
    pairs = devices // 2
    extra = NB - devices
    pair_key, bit_key, rank_key, block_key = jax.random.split(key, 4)
    pair_order = jax.random.permutation(pair_key, pairs).astype(jnp.int32)
    bits = jax.random.randint(bit_key, (pairs,), 0, 2).astype(jnp.int32)
    chosen = 2 * pair_order[:NREF] + bits[:NREF]
    marked = jnp.zeros((devices,), jnp.int32).at[chosen].set(1)
    ranks = jax.random.permutation(rank_key, devices).astype(jnp.int32)
    scores = ranks + devices * (1 - marked)
    dev_order = jnp.argsort(scores, stable=True).astype(jnp.int32)
    assign = jnp.concatenate([dev_order, dev_order[NREF:NREF + extra]])
    block_order = jax.random.permutation(block_key, NB).astype(jnp.int32)
    owners = jnp.zeros((NB,), jnp.int32).at[block_order].set(assign)
    flags = jnp.zeros((NB,), jnp.int32).at[block_order[:NREF]].set(1)
    return (owners, flags)


def factor_draw(key, floor, weight, spread):
    row_key, entry_key = jax.random.split(key)
    rows = jnp.exp(jax.random.uniform(row_key, (SLOTS, B, 1), jnp.float32, 0.0, math.log(spread)))
    entries = jax.random.normal(entry_key, (SLOTS, B, B), jnp.float32) * rows
    gram = jnp.einsum('sij,skj->sik', entries, entries, precision=lax.Precision.HIGHEST) / B
    return floor * jnp.eye(B, dtype=jnp.float32)[None] + weight * gram


def draw_owner(key, part):
    return owner_table(key)[0]


def draw_refresh(key, part):
    return owner_table(key)[1]


def draw_stats_left(key, part):
    key = jax.random.fold_in(key, 11)
    spread = 1.0
    return factor_draw(key, 0.05, 1.0, spread)


def draw_stats_right(key, part):
    key = jax.random.fold_in(key, 12)
    spread = 1.0
    return factor_draw(key, 0.05, 1.0, spread)


def draw_roots_left(key, part):
    key = jax.random.fold_in(key, 13)
    spread = 1.0
    return factor_draw(key, 0.6, 0.4, spread)


def draw_roots_right(key, part):
    key = jax.random.fold_in(key, 14)
    spread = 1.0
    return factor_draw(key, 0.6, 0.4, spread)


def shard_levels(rng, dims, cuts, least, high):
    factor_of, own = 1.0, jax.random.fold_in(rng, 6)
    for dim, blocks in cuts:
        draws = jnp.exp(jax.random.uniform(jax.random.fold_in(own, dim), (blocks,), jnp.float32, least / len(cuts), high / len(cuts)))
        factor_of = factor_of * jnp.repeat(draws, dims[dim] // blocks).reshape([-1 if axis == dim else 1 for axis in range(len(dims))])
    return factor_of


def normal_values(rng, dims, width, most, pieces=(), kind=jnp.bfloat16):
    values = jax.random.normal(rng, dims, jnp.float32) * width
    if len(pieces) > 0:
        values = shard_levels(rng, dims, pieces, -0.22, 0.18) * values
    return jnp.clip(values, min=-most, max=most).astype(kind)


def setup_inputs(seed: int = 0) -> dict:
    key_of = jax.random.split(jax.random.key(seed), 9)
    return {
        "grad_partial": normal_values(key_of[0], (N_DP, NB, B, B), 0.5, 6.0, ((0, 4), (2, 32)), jnp.float32),
        "params": normal_values(key_of[1], (NB, B, B), 0.05, 0.75, ((1, 32),)),
        "stats_left": draw_stats_left(jax.random.fold_in(key_of[8], 71), 0),
        "stats_right": draw_stats_right(jax.random.fold_in(key_of[8], 71), 0),
        "roots_left": draw_roots_left(jax.random.fold_in(key_of[8], 71), 0),
        "roots_right": draw_roots_right(jax.random.fold_in(key_of[8], 71), 0),
        "owner": draw_owner(jax.random.fold_in(key_of[8], 71), 0),
        "refresh": draw_refresh(jax.random.fold_in(key_of[8], 71), 0),
    }


beta_decay = 0.9
learn_rate = 0.2
epsilon = 1e-06

def high_dot(left, right):
    return jnp.dot(left, right, precision=lax.Precision.HIGHEST, preferred_element_type=jnp.float32)

def newton_root(matrix):
    ident = jnp.eye(matrix.shape[0], dtype=jnp.float32)
    scale = jnp.sqrt(jnp.sum(matrix * matrix) + epsilon)
    mixed = matrix / scale
    result = ident * scale ** (-0.25)
    for sweep in range(ITERS):
        factor = (5.0 * ident - mixed) * 0.25
        result = high_dot(result, factor)
        square = high_dot(factor, factor)
        mixed = high_dot(high_dot(square, square), mixed)
    return result

def update_block(items):
    grad, old_left, old_right, keep_left, keep_right, flag = items
    left = beta_decay * old_left + (1.0 - beta_decay) * high_dot(grad, grad.T) / B
    right = beta_decay * old_right + (1.0 - beta_decay) * high_dot(grad.T, grad) / B
    inv_left, inv_right = lax.cond(flag > 0, lambda: (newton_root(left), newton_root(right)), lambda: (keep_left, keep_right))
    precond = high_dot(high_dot(inv_left, grad), inv_right)
    ratio = jnp.sqrt(jnp.sum(grad * grad)) / jnp.sqrt(jnp.sum(precond * precond) + epsilon)
    step = (learn_rate * precond * ratio).astype(jnp.bfloat16)
    return (left, right, step)

def reference(grad_partial, params, stats_left, stats_right, roots_left, roots_right, owner, refresh):
    blocks = jnp.arange(NB, dtype=jnp.int32)
    same = (owner[:, None] == owner[None, :]) & (blocks[None, :] < blocks[:, None])
    slot = owner * CAP + lax.optimization_barrier(jnp.sum(same.astype(jnp.int32), axis=1)).astype(jnp.int32)
    grad = lax.optimization_barrier(jnp.sum(grad_partial, axis=0))
    left, right, step = lax.map(update_block, (grad, stats_left[slot], stats_right[slot], roots_left[slot], roots_right[slot], refresh))
    new_params = (params.astype(jnp.float32) - step.astype(jnp.float32)).astype(jnp.bfloat16)
    new_left = jnp.zeros((SLOTS, B, B), jnp.float32).at[slot].set(left)
    new_right = jnp.zeros((SLOTS, B, B), jnp.float32).at[slot].set(right)
    return (new_params, new_left, new_right)
```

```python
import jax
import jax.numpy as jnp
from jax import lax
from jax.experimental import pallas as pl
from jax.experimental.pallas import tpu as pltpu
from jax.sharding import PartitionSpec as P

MESH = pl.DeviceIdType.MESH
F32 = jnp.float32
BF16 = jnp.bfloat16

beta_decay = 0.9
learn_rate = 0.2
epsilon = 1e-06
ITERS = 6

PLANES = 4
SIDE = 4
COLS = SIDE * SIDE
CORES = 2
CAP = 2
ROWS = 16
WIDTH = 512
GROUP = PLANES * CAP * COLS
HOPS = (2, 1, 3)
TURNS = tuple((dy, dx) for dy in range(SIDE) for dx in range(SIDE) if (dy, dx) != (0, 0))


class Place:
    def __init__(self):
        dp = lax.axis_index("dp")
        fsdp = lax.axis_index("fsdp")
        self.core = lax.rem(dp, 2)
        self.plane = (dp // 2) * 2 + fsdp // COLS
        self.low = fsdp // COLS
        self.col = lax.rem(fsdp, COLS)
        self.y = self.col // SIDE
        self.x = lax.rem(self.col, SIDE)

    def at(self, core, plane, col):
        return ((plane // 2) * 2 + core, lax.rem(plane, 2) * COLS + col)

    def sibling(self):
        return self.at(1 - self.core, self.plane, self.col)

    def up(self, hop):
        return lax.rem(self.plane + hop, PLANES)

    def turn(self, turn):
        dy, dx = turn
        return lax.rem(self.y + dy, SIDE) * SIDE + lax.rem(self.x + dx, SIDE)


def greet(place):
    barrier = pltpu.get_barrier_semaphore()
    partners = [place.sibling()]
    partners += [place.at(place.core, place.up(hop), place.col) for hop in HOPS]
    partners += [place.at(place.core, place.plane, place.turn(turn)) for turn in TURNS]
    for partner in partners:
        pl.semaphore_signal(barrier, inc=1, device_id=partner, device_id_type=MESH)
    pl.semaphore_wait(barrier, len(partners))


def remote(src, dst, send, recv, device):
    return pltpu.make_async_remote_copy(
        src_ref=src, dst_ref=dst, send_sem=send, recv_sem=recv, device_id=device, device_id_type=MESH
    )


def gather_kernel(
    block_ref, grad_ref, out_ref, held,
    core_out, core_in, plane_out, plane_in, own, col_out,
    core_s, core_r, plane_s, plane_r, col_s, col_r,
):
    place = Place()
    greet(place)
    chunks = [(slot, hop) for slot in range(CAP) for hop in HOPS + (0,)]

    def base(core, hop, slot):
        return (core * PLANES + place.up(hop)) * CAP * COLS + slot * COLS

    core_copies = []
    for k, (slot, hop) in enumerate(chunks):
        start = base(1 - place.core, hop, slot)

        def pack(e, carry, k=k, start=start):
            core_out[k, e] = grad_ref[block_ref[start + e]]
            return carry

        lax.fori_loop(0, COLS, pack, 0, unroll=4)
        copy = remote(core_out.at[k], core_in.at[k], core_s.at[k], core_r.at[k], place.sibling())
        copy.start()
        core_copies.append(copy)

    plane_copies = {}
    col_copies = []
    for slot in range(CAP):
        for hop in HOPS + (0,):
            k = chunks.index((slot, hop))
            core_copies[k].wait_recv()
            start = base(place.core, hop, slot)
            if hop:
                h = HOPS.index(hop)

                def add(e, carry, k=k, start=start, slot=slot, h=h):
                    total = grad_ref[block_ref[start + e]] + core_in[k, e]
                    plane_out[slot, h, e] = total.astype(BF16)
                    return carry

                lax.fori_loop(0, COLS, add, 0, unroll=4)
                copy = remote(
                    plane_out.at[slot, h], plane_in.at[slot, h], plane_s.at[slot, h], plane_r.at[slot, h],
                    place.at(place.core, place.up(hop), place.col),
                )
                copy.start()
                plane_copies[slot, h] = copy
            else:

                def keep(e, carry, k=k, start=start, slot=slot):
                    own[slot, e] = grad_ref[block_ref[start + e]] + core_in[k, e]
                    return carry

                lax.fori_loop(0, COLS, keep, 0, unroll=4)

    for slot in range(CAP):
        for h in range(len(HOPS)):
            plane_copies[slot, h].wait_recv()

        def fold(e, carry, slot=slot):
            same = own[slot, e] + plane_in[slot, 0, e].astype(F32)
            other = plane_in[slot, 1, e].astype(F32) + plane_in[slot, 2, e].astype(F32)
            col_out[slot, e, place.low] = same.astype(BF16)
            col_out[slot, e, 1 - place.low] = other.astype(BF16)
            return carry

        lax.fori_loop(0, COLS, fold, 0, unroll=2)
        for t, turn in enumerate(TURNS):
            col = place.turn(turn)
            copy = remote(
                col_out.at[slot, col], held.at[slot, :, place.col], col_s.at[slot, t], col_r.at[slot, t],
                place.at(place.core, place.plane, col),
            )
            copy.start()
            col_copies.append(copy)
        held[slot, :, place.col] = col_out[slot, place.col]

    for copy in col_copies:
        copy.wait_recv()
    out_ref[...] = held[...]
    for copy in core_copies + list(plane_copies.values()) + col_copies:
        copy.wait_send()


def dot(left, right):
    return jnp.dot(left, right, preferred_element_type=F32)


def dot_t(left, right, dims):
    return lax.dot_general(left, right, ((dims, dims), ((), ())), preferred_element_type=F32)


def halves(value):
    high = value.astype(BF16)
    return high, (value - high.astype(F32)).astype(BF16)


def total_square(value):
    return jnp.sum(value * value, axis=(0, 1), keepdims=True)


def root_into(factor_ref, result, mixed):
    factor = factor_ref[...]
    scale = jnp.sqrt(total_square(factor) + epsilon)
    start = factor / scale
    mixed[...] = start
    row = lax.broadcasted_iota(jnp.int32, start.shape, 0)
    column = lax.broadcasted_iota(jnp.int32, start.shape, 1)
    ident = jnp.where(row == column, 1.0, 0.0).astype(F32)
    result[...] = lax.rsqrt(jnp.sqrt(scale)) * (1.25 * ident - 0.25 * start)


def root_sweep(result, mixed):
    now = mixed[...]
    low = now.astype(BF16)
    edge = (dot(low, low) - 10.0 * now) * (1.0 / 16.0)
    edge_low = edge.astype(BF16)
    fourth = dot(edge_low, edge_low) + 3.125 * edge
    now = (625.0 / 256.0) * now + dot(fourth.astype(BF16), low)
    mixed[...] = now
    held = result[...]
    result[...] = 1.25 * held - 0.25 * dot(held.astype(BF16), now.astype(BF16))


def update_kernel(
    flags_ref, grad_ref, stats_left, stats_right, roots_left, roots_right,
    step_ref, new_left, new_right, inv_left, inv_right, mixed_left, mixed_right,
):
    def owned(slot, carry):
        grad = grad_ref[slot]
        live = jnp.where(flags_ref[slot] > 0, 1.0, 0.0)
        scale = (1.0 - beta_decay) / WIDTH
        new_left[slot] = live * (beta_decay * stats_left[slot] + scale * dot_t(grad, grad, (1,)))
        new_right[slot] = live * (beta_decay * stats_right[slot] + scale * dot_t(grad, grad, (0,)))
        inv_left[...] = roots_left[slot]
        inv_right[...] = roots_right[slot]

        @pl.when(flags_ref[CAP + slot] > 0)
        def fresh():
            root_into(new_left.at[slot], inv_left, mixed_left)
            root_into(new_right.at[slot], inv_right, mixed_right)

            def sweep(i, carry):
                root_sweep(inv_left, mixed_left)
                root_sweep(inv_right, mixed_right)
                return carry

            lax.fori_loop(0, ITERS - 1, sweep, 0)

        left_high, left_low = halves(inv_left[...])
        inner_high, inner_low = halves(dot(left_high, grad) + dot(left_low, grad))
        right_high, right_low = halves(inv_right[...])
        precond = dot(inner_high, right_high) + (dot(inner_low, right_high) + dot(inner_high, right_low))
        ratio = jnp.sqrt(total_square(grad.astype(F32))) / jnp.sqrt(total_square(precond) + epsilon)
        step_ref[slot] = (learn_rate * precond * ratio).astype(BF16)
        return carry

    lax.fori_loop(0, CAP, owned, 0)


def spread_kernel(step_ref, out_ref, rows, col_s, col_r, plane_s, plane_r, core_s, core_r):
    place = Place()
    greet(place)
    copies = []
    col_copies = {}
    for slot in range(CAP):
        for t, turn in enumerate(TURNS):
            col = place.turn(turn)
            copy = remote(
                step_ref.at[slot, :, col], rows.at[slot, place.col], col_s.at[slot, t], col_r.at[slot, t],
                place.at(place.core, place.plane, col),
            )
            copy.start()
            col_copies[slot, t] = copy
        rows[slot, place.col] = step_ref[slot, :, place.col]

    plane_copies = {}
    for slot in range(CAP):
        for t in range(len(TURNS)):
            col_copies[slot, t].wait_recv()
        for h, hop in enumerate(HOPS):
            plane = place.up(hop)
            copy = remote(
                rows.at[slot, :, lax.rem(plane, 2)], out_ref.at[place.core, place.plane, slot],
                plane_s.at[slot, h], plane_r.at[slot, h], place.at(place.core, plane, place.col),
            )
            copy.start()
            plane_copies[slot, h] = copy
        out_ref[place.core, place.plane, slot] = rows[slot, :, place.low]

    core_copies = []
    for slot in range(CAP):
        for h, hop in ((len(HOPS), 0),) + tuple(enumerate(HOPS)):
            if hop:
                plane_copies[slot, h].wait_recv()
            plane = place.up(PLANES - hop)
            here = out_ref.at[place.core, plane, slot]
            copy = remote(here, here, core_s.at[slot, h], core_r.at[slot, h], place.sibling())
            copy.start()
            core_copies.append(copy)
    for copy in core_copies:
        copy.wait_recv()
    for copy in core_copies + list(plane_copies.values()) + list(col_copies.values()):
        copy.wait_send()


def apply_kernel(entry_ref, step_ref, params_ref, out_ref):
    def one(b, carry):
        step = step_ref[entry_ref[b]].astype(F32)
        out_ref[b] = (params_ref[b].astype(F32) - step).astype(BF16)
        return carry

    lax.fori_loop(0, params_ref.shape[0], one, 0, unroll=4)


SMEM = pl.BlockSpec(memory_space=pltpu.SMEM)
VMEM = pl.BlockSpec(memory_space=pltpu.VMEM)
LIMIT = 56 << 20


def body(grad_partial, params, stats_left, stats_right, roots_left, roots_right, owner, refresh):
    count = params.shape[0]
    slots = CORES * GROUP
    blocks = jnp.arange(count, dtype=jnp.int32)
    same = (owner[:, None] == owner[None, :]) & (blocks[None, :] < blocks[:, None])
    slot_of = owner * CAP + jnp.sum(same.astype(jnp.int32), axis=1)
    match = slot_of[None, :] == jnp.arange(slots, dtype=jnp.int32)[:, None]
    block_of = jnp.sum(jnp.where(match, blocks[None, :], 0), axis=1)
    filled = jnp.sum(match.astype(jnp.int32), axis=1)
    fresh = jnp.sum(jnp.where(match, refresh[None, :], 0), axis=1)
    device = lax.axis_index("dp") * lax.axis_size("fsdp") + lax.axis_index("fsdp")
    flags = jnp.concatenate(
        [lax.dynamic_slice_in_dim(filled, device * CAP, CAP), lax.dynamic_slice_in_dim(fresh, device * CAP, CAP)]
    )
    packed = block_of.reshape(2, CORES, 2, COLS, CAP).transpose(1, 0, 2, 4, 3).reshape(slots)
    device_of, rank = slot_of // CAP, slot_of % CAP
    z_hi, core, z_lo, col = device_of // 64, device_of // 32 % 2, device_of // COLS % 2, device_of % COLS
    entry = ((core * PLANES + 2 * z_hi + z_lo) * CAP + rank) * COLS + col

    dma = pltpu.SemaphoreType.DMA
    hops, turns = len(HOPS), len(TURNS)
    gradient = pl.pallas_call(
        gather_kernel,
        name="gather",
        out_shape=jax.ShapeDtypeStruct((CAP, 2, COLS, ROWS, WIDTH), BF16),
        in_specs=[SMEM, VMEM],
        out_specs=VMEM,
        scratch_shapes=[
            pltpu.VMEM((CAP, 2, COLS, ROWS, WIDTH), BF16),
            pltpu.VMEM((CAP * PLANES, COLS, ROWS, WIDTH), F32),
            pltpu.VMEM((CAP * PLANES, COLS, ROWS, WIDTH), F32),
            pltpu.VMEM((CAP, hops, COLS, ROWS, WIDTH), BF16),
            pltpu.VMEM((CAP, hops, COLS, ROWS, WIDTH), BF16),
            pltpu.VMEM((CAP, COLS, ROWS, WIDTH), F32),
            pltpu.VMEM((CAP, COLS, 2, ROWS, WIDTH), BF16),
            dma((CAP * PLANES,)), dma((CAP * PLANES,)),
            dma((CAP, hops)), dma((CAP, hops)),
            dma((CAP, turns)), dma((CAP, turns)),
        ],
        compiler_params=pltpu.CompilerParams(collective_id=0, has_side_effects=True, vmem_limit_bytes=LIMIT),
    )(packed, grad_partial[0])

    steps, new_left, new_right = pl.pallas_call(
        update_kernel,
        name="update",
        out_shape=[
            jax.ShapeDtypeStruct((CAP, WIDTH, WIDTH), BF16),
            jax.ShapeDtypeStruct((CAP, WIDTH, WIDTH), F32),
            jax.ShapeDtypeStruct((CAP, WIDTH, WIDTH), F32),
        ],
        in_specs=[SMEM] + [VMEM] * 5,
        out_specs=[VMEM] * 3,
        scratch_shapes=[pltpu.VMEM((WIDTH, WIDTH), F32)] * 4,
        compiler_params=pltpu.CompilerParams(vmem_limit_bytes=LIMIT),
    )(flags, gradient.reshape(CAP, WIDTH, WIDTH), stats_left, stats_right, roots_left, roots_right)

    every = pl.pallas_call(
        spread_kernel,
        name="spread",
        out_shape=jax.ShapeDtypeStruct((CORES, PLANES, CAP, COLS, ROWS, WIDTH), BF16),
        in_specs=[VMEM],
        out_specs=VMEM,
        scratch_shapes=[
            pltpu.VMEM((CAP, COLS, 2, ROWS, WIDTH), BF16),
            dma((CAP, turns)), dma((CAP, turns)),
            dma((CAP, hops)), dma((CAP, hops)),
            dma((CAP, hops + 1)), dma((CAP, hops + 1)),
        ],
        compiler_params=pltpu.CompilerParams(collective_id=1, has_side_effects=True, vmem_limit_bytes=LIMIT),
    )(steps.reshape(CAP, 2, COLS, ROWS, WIDTH))

    new_params = pl.pallas_call(
        apply_kernel,
        name="apply",
        out_shape=jax.ShapeDtypeStruct(params.shape, BF16),
        in_specs=[SMEM, VMEM, VMEM],
        out_specs=VMEM,
        compiler_params=pltpu.CompilerParams(vmem_limit_bytes=LIMIT),
    )(entry, every.reshape(slots, ROWS, WIDTH), params)
    return (new_params, new_left, new_right)


def solution(mesh):
    in_specs = (
        P("dp", None, "fsdp", None),
        P(None, "fsdp", None),
        P(("dp", "fsdp"), None, None),
        P(("dp", "fsdp"), None, None),
        P(("dp", "fsdp"), None, None),
        P(("dp", "fsdp"), None, None),
        P(),
        P(),
    )
    out_specs = (
        P(None, "fsdp", None),
        P(("dp", "fsdp"), None, None),
        P(("dp", "fsdp"), None, None),
    )
    return jax.shard_map(body, mesh=mesh, in_specs=in_specs, out_specs=out_specs, check_vma=False)
```

```python
import jax
import jax.numpy as jnp
from jax import lax
from jax.experimental import pallas as pl
from jax.experimental.pallas import tpu as pltpu
from jax.sharding import PartitionSpec as P

MESH = pl.DeviceIdType.MESH
F32 = jnp.float32
BF16 = jnp.bfloat16

beta_decay = 0.9
learn_rate = 0.2
epsilon = 1e-06
ITERS = 6

PLANES = 4
SIDE = 4
COLS = SIDE * SIDE
CORES = 2
CAP = 2
ROWS = 16
WIDTH = 512
SLOTS = CORES * PLANES * CAP * COLS
HOPS = (1, 3, 2)
CHUNKS = HOPS + (0,)


class Place:
    def __init__(self):
        dp = lax.axis_index("dp")
        fsdp = lax.axis_index("fsdp")
        self.core = lax.rem(dp, 2)
        self.plane = (dp // 2) * 2 + fsdp // COLS
        self.low = fsdp // COLS
        self.col = lax.rem(fsdp, COLS)

    def at(self, core, plane, col):
        return ((plane // 2) * 2 + core, lax.rem(plane, 2) * COLS + col)

    def sibling(self):
        return self.at(1 - self.core, self.plane, self.col)

    def up(self, hop):
        return lax.rem(self.plane + hop, PLANES)

    def above(self, hop):
        return self.at(self.core, self.up(hop), self.col)

    def turn(self, t):
        y, x = self.col // SIDE, lax.rem(self.col, SIDE)
        return lax.rem(y + t // SIDE, SIDE) * SIDE + lax.rem(x + lax.rem(t, SIDE), SIDE)

    def half(self, which):
        return 1 - self.low if which == 0 else self.low


def greet(place):
    barrier = pltpu.get_barrier_semaphore()
    partners = [place.sibling()] + [place.above(hop) for hop in HOPS]
    partners += [place.at(place.core, place.plane, place.turn(t)) for t in range(1, COLS)]
    for partner in partners:
        pl.semaphore_signal(barrier, inc=1, device_id=partner, device_id_type=MESH)
    pl.semaphore_wait(barrier, len(partners))


def remote(src, dst, send, recv, device):
    return pltpu.make_async_remote_copy(
        src_ref=src, dst_ref=dst, send_sem=send, recv_sem=recv, device_id=device, device_id_type=MESH
    )


def dot(left, right):
    return jnp.dot(left, right, preferred_element_type=F32)


def dot_t(left, right, dims):
    return lax.dot_general(left, right, ((dims, dims), ((), ())), preferred_element_type=F32)


def halves(value):
    high = value.astype(BF16)
    return high, (value - high.astype(F32)).astype(BF16)


def total_square(value):
    return jnp.sum(value * value, axis=(0, 1), keepdims=True)


def root_start(factor, result, mixed):
    scale = jnp.sqrt(total_square(factor) + epsilon)
    start = factor / scale
    mixed[...] = start
    row = lax.broadcasted_iota(jnp.int32, start.shape, 0)
    column = lax.broadcasted_iota(jnp.int32, start.shape, 1)
    ident = jnp.where(row == column, 1.0, 0.0).astype(F32)
    result[...] = lax.rsqrt(jnp.sqrt(scale)) * (1.25 * ident - 0.25 * start)


def root_sweep(result, mixed):
    now = mixed[...]
    low = now.astype(BF16)
    edge = (dot(low, low) - 10.0 * now) * (1.0 / 16.0)
    edge_low = edge.astype(BF16)
    fourth = dot(edge_low, edge_low) + 3.125 * edge
    now = (625.0 / 256.0) * now + dot(fourth.astype(BF16), low)
    mixed[...] = now
    held = result[...]
    result[...] = 1.25 * held - 0.25 * dot(held.astype(BF16), now.astype(BF16))


def scaled_step(precond, grad):
    ratio = jnp.sqrt(total_square(grad.astype(F32))) / jnp.sqrt(total_square(precond) + epsilon)
    return (learn_rate * precond * ratio).astype(BF16)


def kept_step(inv_left, grad, inv_right):
    left_high, left_low = halves(inv_left)
    inner_high, inner_low = halves(dot(left_high, grad) + dot(left_low, grad))
    right_high, right_low = halves(inv_right)
    precond = dot(inner_high, right_high) + (dot(inner_low, right_high) + dot(inner_high, right_low))
    return scaled_step(precond, grad)


def whole_kernel(
    block_ref, entry_ref, flags_ref,
    grad_hbm, params_hbm, stats_left, stats_right, roots_left, roots_right,
    out_params, out_left, out_right,
    grad_ref, params_ref, result_ref, keep, gram, inverse, mixed,
    core_out, core_in, plane_out, plane_in, own, col_out, held, step, rows, every,
    local_sems, core_s, core_r, plane_s, plane_r, col_s, col_r,
    plane_s2, plane_r2, col_s2, col_r2, core_s2, core_r2,
):
    place = Place()
    load_grad = pltpu.make_async_copy(grad_hbm.at[0], grad_ref, local_sems.at[0])
    load_grad.start()
    greet(place)
    load_grad.wait()

    def base(core, hop, slot):
        return (core * PLANES + place.up(hop)) * CAP * COLS + slot * COLS

    core_copies = {}
    plane_copies = {}

    def pack(slot):
        for h, hop in enumerate(CHUNKS):
            start = base(1 - place.core, hop, slot)

            def one(e, carry, h=h, start=start):
                core_out[slot, h, e] = grad_ref[block_ref[start + e]]
                return carry

            lax.fori_loop(0, COLS, one, 0, unroll=4)
            copy = remote(
                core_out.at[slot, h], core_in.at[slot, h], core_s.at[slot, h], core_r.at[slot, h], place.sibling()
            )
            copy.start()
            core_copies[slot, h] = copy

    def add(slot, send):
        for h, hop in enumerate(CHUNKS):
            core_copies[slot, h].wait_recv()
            start = base(place.core, hop, slot)

            def one(e, carry, h=h, hop=hop, start=start):
                total = grad_ref[block_ref[start + e]] + core_in[slot, h, e]
                if hop:
                    plane_out[slot, h, e] = total.astype(BF16)
                else:
                    own[slot, e] = total
                return carry

            lax.fori_loop(0, COLS, one, 0, unroll=4)
            if hop:
                plane_copies[slot, h] = remote(
                    plane_out.at[slot, h], plane_in.at[slot, h], plane_s.at[slot, h], plane_r.at[slot, h],
                    place.above(hop),
                )
                if send:
                    plane_copies[slot, h].start()

    def col_copy(slot, which, t):
        col, half = place.turn(t), place.half(which)
        return remote(
            col_out.at[slot, half, col], held.at[slot, half, place.col],
            col_s.at[slot, which, t], col_r.at[slot, which, t], place.at(place.core, place.plane, col),
        )

    def fold(slot, which):
        half = place.half(which)

        def one(e, carry):
            if which == 0:
                total = plane_in[slot, 0, e].astype(F32) + plane_in[slot, 1, e].astype(F32)
            else:
                total = own[slot, e] + plane_in[slot, 2, e].astype(F32)
            col_out[slot, half, e] = total.astype(BF16)
            return carry

        lax.fori_loop(0, COLS, one, 0, unroll=4)

        def send(t, carry):
            col_copy(slot, which, t).start()
            return carry

        lax.fori_loop(1, COLS, send, 0)
        held[slot, half, place.col] = col_out[slot, half, place.col]

    def col_wait(slot):
        for which in range(2):

            def one(t, carry):
                col_copy(slot, which, t).wait_recv()
                return carry

            lax.fori_loop(1, COLS, one, 0)

    def back_copy(slot, which, t):
        col, half = place.turn(t), place.half(which)
        return remote(
            step.at[slot, half, col], rows.at[slot, half, place.col],
            col_s2.at[slot, which, t], col_r2.at[slot, which, t], place.at(place.core, place.plane, col),
        )

    def back_send(slot):
        for which in range(2):

            def one(t, carry):
                back_copy(slot, which, t).start()
                return carry

            lax.fori_loop(1, COLS, one, 0)
        rows[slot, :, place.col] = step[slot, :, place.col]

    back_planes = {}
    back_cores = {}

    def region(plane, slot):
        return every.at[pl.ds(((place.core * PLANES + plane) * CAP + slot) * COLS, COLS)]

    def back_core(slot, h, plane):
        here = region(plane, slot)
        copy = remote(here, here, core_s2.at[slot, h], core_r2.at[slot, h], place.sibling())
        copy.start()
        back_cores[slot, h] = copy

    def back_up(slot):
        for which in range(2):

            def one(t, carry):
                back_copy(slot, which, t).wait_recv()
                return carry

            lax.fori_loop(1, COLS, one, 0)
            for h, hop in enumerate(HOPS):
                if (hop == 2) == (which == 1):
                    copy = remote(
                        rows.at[slot, place.half(which)], region(place.plane, slot),
                        plane_s2.at[slot, h], plane_r2.at[slot, h], place.above(hop),
                    )
                    copy.start()
                    back_planes[slot, h] = copy
        region(place.plane, slot)[...] = rows[slot, place.low]
        back_core(slot, len(HOPS), place.plane)

    def back_over(slot):
        for h, hop in enumerate(HOPS):
            back_planes[slot, h].wait_recv()
            back_core(slot, h, place.up(PLANES - hop))

    pack(0)
    add(0, True)
    loads = []
    for i, (src, dst) in enumerate(
        ((roots_left, keep.at[0]), (roots_right, keep.at[1]), (stats_left, gram.at[0]), (stats_right, gram.at[1]),
         (params_hbm, params_ref))
    ):
        copy = pltpu.make_async_copy(src, dst, local_sems.at[1 + i])
        copy.start()
        loads.append(copy)
    pack(1)
    add(1, False)
    plane_copies[0, 0].wait_recv()
    plane_copies[0, 1].wait_recv()
    fold(0, 0)
    plane_copies[0, 2].wait_recv()
    for h in range(len(HOPS)):
        plane_copies[1, h].start()
    fold(0, 1)
    for copy in loads:
        copy.wait()

    def grad_of(slot):
        return held[slot].reshape(WIDTH, WIDTH)

    def put_step(slot, value):
        step[slot] = value.reshape(2, COLS, ROWS, WIDTH)

    stores = []

    def factors(slot):
        grad = grad_of(slot)
        live = jnp.where(flags_ref[slot] > 0, 1.0, 0.0)
        scale = (1.0 - beta_decay) / WIDTH
        for side, dims in enumerate(((1,), (0,))):
            gram[side, slot] = live * (beta_decay * gram[side, slot] + scale * dot_t(grad, grad, dims))
        for side, out in enumerate((out_left, out_right)):
            copy = pltpu.make_async_copy(gram.at[side, slot], out.at[slot], local_sems.at[6 + 2 * slot + side])
            copy.start()
            stores.append(copy)

    def sweeps(count):
        def one(i, carry):
            root_sweep(inverse.at[0], mixed.at[0])
            root_sweep(inverse.at[1], mixed.at[1])
            return carry

        lax.fori_loop(0, count, one, 0)

    col_wait(0)
    put_step(0, kept_step(keep[0, 0], grad_of(0), keep[1, 0]))
    back_send(0)
    factors(0)
    for side in range(2):
        root_start(gram[side, 0], inverse.at[side], mixed.at[side])
    plane_copies[1, 0].wait_recv()
    plane_copies[1, 1].wait_recv()
    fold(1, 0)
    plane_copies[1, 2].wait_recv()
    fold(1, 1)
    sweeps(2)
    back_up(0)
    sweeps(2)
    col_wait(1)
    kept = kept_step(keep[0, 1], grad_of(1), keep[1, 1])
    put_step(1, kept)
    sweeps(1)
    grad = grad_of(0)
    inner = dot(inverse[0].astype(BF16), grad)
    fresh = scaled_step(dot(inner.astype(BF16), inverse[1].astype(BF16)), grad)
    late = step[1].reshape(WIDTH, WIDTH)
    put_step(1, jnp.where(flags_ref[CAP] > 0, fresh.astype(F32), late.astype(F32)).astype(BF16))
    back_send(1)
    factors(1)
    back_over(0)
    back_up(1)
    back_over(1)
    for copy in back_cores.values():
        copy.wait_recv()

    parts = 4
    count = params_ref.shape[0] // parts
    for part in range(parts):

        def one(b, carry):
            change = every[entry_ref[b]].astype(F32)
            result_ref[b] = (params_ref[b].astype(F32) - change).astype(BF16)
            return carry

        lax.fori_loop(part * count, (part + 1) * count, one, 0, unroll=4)
        span = pl.ds(part * count, count)
        copy = pltpu.make_async_copy(result_ref.at[span], out_params.at[span], local_sems.at[10 + part])
        copy.start()
        stores.append(copy)

    for copy in stores:
        copy.wait()
    for copy in list(core_copies.values()) + list(plane_copies.values()):
        copy.wait_send()
    for copy in list(back_planes.values()) + list(back_cores.values()):
        copy.wait_send()
    for slot in range(CAP):
        for which in range(2):

            def done(t, carry):
                col_copy(slot, which, t).wait_send()
                back_copy(slot, which, t).wait_send()
                return carry

            lax.fori_loop(1, COLS, done, 0)


SMEM = pl.BlockSpec(memory_space=pltpu.SMEM)
ANY = pl.BlockSpec(memory_space=pl.ANY)


def body(grad_partial, params, stats_left, stats_right, roots_left, roots_right, owner, refresh):
    count = params.shape[0]
    blocks = jnp.arange(count, dtype=jnp.int32)
    same = (owner[:, None] == owner[None, :]) & (blocks[None, :] < blocks[:, None])
    rank = jnp.sum(same.astype(jnp.int32), axis=1)
    slot_of = owner * CAP + rank
    match = slot_of[None, :] == jnp.arange(SLOTS, dtype=jnp.int32)[:, None]
    block_of = jnp.sum(jnp.where(match, blocks[None, :], 0), axis=1)
    filled = jnp.sum(match.astype(jnp.int32), axis=1)
    fresh = jnp.sum(jnp.where(match, refresh[None, :], 0), axis=1)
    device = lax.axis_index("dp") * lax.axis_size("fsdp") + lax.axis_index("fsdp")
    flags = jnp.concatenate(
        [lax.dynamic_slice_in_dim(filled, device * CAP, CAP), lax.dynamic_slice_in_dim(fresh, device * CAP, CAP)]
    )
    packed = block_of.reshape(2, CORES, 2, COLS, CAP).transpose(1, 0, 2, 4, 3).reshape(SLOTS)
    z_hi, core, z_lo, col = owner // 64, owner // 32 % 2, owner // COLS % 2, owner % COLS
    back = rank + refresh
    entry = ((core * PLANES + 2 * z_hi + z_lo) * CAP + back) * COLS + col

    dma = pltpu.SemaphoreType.DMA
    hops = len(HOPS)
    piece = (COLS, ROWS, WIDTH)
    new_params, new_left, new_right = pl.pallas_call(
        whole_kernel,
        name="whole",
        out_shape=[
            jax.ShapeDtypeStruct(params.shape, BF16),
            jax.ShapeDtypeStruct((CAP, WIDTH, WIDTH), F32),
            jax.ShapeDtypeStruct((CAP, WIDTH, WIDTH), F32),
        ],
        in_specs=[SMEM] * 3 + [ANY] * 6,
        out_specs=[ANY] * 3,
        scratch_shapes=[
            pltpu.VMEM((count, ROWS, WIDTH), F32),
            pltpu.VMEM((count, ROWS, WIDTH), BF16),
            pltpu.VMEM((count, ROWS, WIDTH), BF16),
            pltpu.VMEM((2, CAP, WIDTH, WIDTH), F32),
            pltpu.VMEM((2, CAP, WIDTH, WIDTH), F32),
            pltpu.VMEM((2, WIDTH, WIDTH), F32),
            pltpu.VMEM((2, WIDTH, WIDTH), F32),
            pltpu.VMEM((CAP, PLANES) + piece, F32),
            pltpu.VMEM((CAP, PLANES) + piece, F32),
            pltpu.VMEM((CAP, hops) + piece, BF16),
            pltpu.VMEM((CAP, hops) + piece, BF16),
            pltpu.VMEM((CAP,) + piece, F32),
            pltpu.VMEM((CAP, 2) + piece, BF16),
            pltpu.VMEM((CAP, 2) + piece, BF16),
            pltpu.VMEM((CAP, 2) + piece, BF16),
            pltpu.VMEM((CAP, 2) + piece, BF16),
            pltpu.VMEM((SLOTS, ROWS, WIDTH), BF16),
            dma((14,)),
            dma((CAP, PLANES)), dma((CAP, PLANES)),
            dma((CAP, hops)), dma((CAP, hops)),
            dma((CAP, 2, COLS)), dma((CAP, 2, COLS)),
            dma((CAP, hops)), dma((CAP, hops)),
            dma((CAP, 2, COLS)), dma((CAP, 2, COLS)),
            dma((CAP, PLANES)), dma((CAP, PLANES)),
        ],
        compiler_params=pltpu.CompilerParams(collective_id=0, has_side_effects=True, vmem_limit_bytes=60 << 20),
    )(packed, entry, flags, grad_partial, params, stats_left, stats_right, roots_left, roots_right)
    return (new_params, new_left, new_right)


def solution(mesh):
    in_specs = (
        P("dp", None, "fsdp", None),
        P(None, "fsdp", None),
        P(("dp", "fsdp"), None, None),
        P(("dp", "fsdp"), None, None),
        P(("dp", "fsdp"), None, None),
        P(("dp", "fsdp"), None, None),
        P(),
        P(),
    )
    out_specs = (
        P(None, "fsdp", None),
        P(("dp", "fsdp"), None, None),
        P(("dp", "fsdp"), None, None),
    )
    return jax.shard_map(body, mesh=mesh, in_specs=in_specs, out_specs=out_specs, check_vma=False)
```

```python
import jax
import jax.numpy as jnp
from jax import lax
from jax.experimental import pallas as pl
from jax.experimental.pallas import tpu as pltpu
from jax.sharding import PartitionSpec as P

MESH = pl.DeviceIdType.MESH
F32 = jnp.float32
BF16 = jnp.bfloat16

beta_decay = 0.9
learn_rate = 0.2
epsilon = 1e-06
ITERS = 6

PLANES = 4
SIDE = 4
COLS = SIDE * SIDE
CORES = 2
CAP = 2
ROWS = 16
WIDTH = 512
SLOTS = CORES * PLANES * CAP * COLS
HOPS = (1, 3, 2)
CHUNKS = HOPS + (0,)
AHEAD, BEHIND, SECOND = range(3)
PARTS = ((0, 0, COLS // 2, 2), (0, COLS // 2, COLS // 2, 2), (1, 0, COLS, 1))


class Place:
    def __init__(self):
        dp = lax.axis_index("dp")
        fsdp = lax.axis_index("fsdp")
        self.core = lax.rem(dp, 2)
        self.plane = (dp // 2) * 2 + fsdp // COLS
        self.low = fsdp // COLS
        self.col = lax.rem(fsdp, COLS)

    def at(self, core, plane, col):
        return ((plane // 2) * 2 + core, lax.rem(plane, 2) * COLS + col)

    def sibling(self):
        return self.at(1 - self.core, self.plane, self.col)

    def up(self, hop):
        return lax.rem(self.plane + hop, PLANES)

    def above(self, hop):
        return self.at(self.core, self.up(hop), self.col)

    def turn(self, t):
        y, x = self.col // SIDE, lax.rem(self.col, SIDE)
        return lax.rem(y + t // SIDE, SIDE) * SIDE + lax.rem(x + lax.rem(t, SIDE), SIDE)

    def half(self, which):
        return 1 - self.low if which == 0 else self.low


def greet(place):
    partners = [place.sibling()] + [place.above(hop) for hop in HOPS]
    partners += [place.at(place.core, place.plane, place.turn(t)) for t in range(1, COLS)]
    for partner in partners:
        pl.semaphore_signal(pltpu.get_barrier_semaphore(), inc=1, device_id=partner, device_id_type=MESH)
    return len(partners)


def spread_order(i):
    return lax.rem(5 * i, COLS)


def count_up(mask, axis):
    return jnp.sum(mask.astype(jnp.int32), axis=axis, keepdims=True)


def index_tables(owner, refresh, device):
    count = owner.shape[1]
    row = lax.broadcasted_iota(jnp.int32, (count, count), 0)
    column = lax.broadcasted_iota(jnp.int32, (count, count), 1)
    owner_down = jnp.sum(jnp.where(row == column, owner, 0), axis=1, keepdims=True)
    refresh_down = jnp.sum(jnp.where(row == column, refresh, 0), axis=1, keepdims=True)
    same = owner_down == owner
    other_down = count_up(((owner_down ^ 1) == owner) & (refresh > 0), 1)
    ahead_down = (refresh_down > 0) | (((owner_down & 1) == 0) & (other_down == 0))
    rank = count_up(same & (row < column), 0)
    rank_down = count_up(same & (column < row), 1)

    def first(own):
        core, plane = (own >> 5) & 1, 2 * (own >> 6) + ((own >> 4) & 1)
        return (core * PLANES + plane) * CAP * COLS

    entry = first(owner) + (rank + refresh) * COLS + (owner & (COLS - 1))
    col_down = owner_down & (COLS - 1)
    pair_down = (col_down >> 1) + jnp.where(ahead_down, 0, COLS // 2)
    place_down = first(owner_down) + jnp.where(rank_down > 0, COLS + col_down, pair_down)
    spot = lax.broadcasted_iota(jnp.int32, (count, SLOTS), 1)
    block = lax.broadcasted_iota(jnp.int32, (count, SLOTS), 0)
    packed = jnp.sum(jnp.where(place_down == spot, block, 0), axis=0, keepdims=True)
    mine = owner == device
    live = [count_up(mine & (rank == slot), 1) for slot in range(CAP)]
    fresh = count_up(mine & (refresh > 0), 1)
    other = count_up((owner == (device ^ 1)) & (refresh > 0), 1)
    ahead = (fresh > 0) | (((device & 1) == 0) & (other == 0))
    return jnp.minimum(packed, count - 1), jnp.minimum(entry, SLOTS - 1), live, fresh, ahead


def remote(src, dst, send, recv, device):
    return pltpu.make_async_remote_copy(
        src_ref=src, dst_ref=dst, send_sem=send, recv_sem=recv, device_id=device, device_id_type=MESH
    )


def dot(left, right):
    return jnp.dot(left, right, preferred_element_type=F32)


def dot_t(left, right, dims):
    return lax.dot_general(left, right, ((dims, dims), ((), ())), preferred_element_type=F32)


def halves(value):
    high = value.astype(BF16)
    return high, (value - high.astype(F32)).astype(BF16)


def total_square(value):
    return jnp.sum(value * value, axis=(0, 1), keepdims=True)


def root_start(factor, result, mixed):
    scale = jnp.sqrt(total_square(factor) + epsilon)
    start = factor / scale
    mixed[...] = start
    row = lax.broadcasted_iota(jnp.int32, start.shape, 0)
    column = lax.broadcasted_iota(jnp.int32, start.shape, 1)
    ident = jnp.where(row == column, 1.0, 0.0).astype(F32)
    result[...] = lax.rsqrt(jnp.sqrt(scale)) * (1.25 * ident - 0.25 * start)


def root_sweep(result, mixed):
    now = mixed[...]
    low = now.astype(BF16)
    edge = (dot(low, low) - 10.0 * now) * (1.0 / 16.0)
    edge_low = edge.astype(BF16)
    fourth = dot(edge_low, edge_low) + 3.125 * edge
    now = (625.0 / 256.0) * now + dot(fourth.astype(BF16), low)
    mixed[...] = now
    held = result[...]
    result[...] = 1.25 * held - 0.25 * dot(held.astype(BF16), now.astype(BF16))


def scaled_step(precond, grad):
    ratio = jnp.sqrt(total_square(grad.astype(F32))) / jnp.sqrt(total_square(precond) + epsilon)
    return (learn_rate * precond * ratio).astype(BF16)


def kept_step(inv_left, grad, inv_right):
    left_high, left_low = halves(inv_left)
    inner_high, inner_low = halves(dot(left_high, grad) + dot(left_low, grad))
    right_high, right_low = halves(inv_right)
    precond = dot(inner_high, right_high) + (dot(inner_low, right_high) + dot(inner_high, right_low))
    return scaled_step(precond, grad)


def whole_kernel(
    owner_hbm, refresh_hbm, grad_hbm, params_hbm, stats_left, stats_right, roots_left, roots_right,
    result_ref, gram,
    owner_ref, refresh_ref, table_vmem, table, grad_ref, keep, inverse, mixed,
    core_out, core_in, plane_out, plane_in, col_out, held, step, rows, every,
    local_sems, core_s, core_r, plane_s, plane_r, col_s, col_r,
    row_s, row_r, up_s, up_r, back_s, back_r, core_s2, core_r2,
):
    place = Place()
    loads = [
        pltpu.make_async_copy(owner_hbm, owner_ref, local_sems.at[7]),
        pltpu.make_async_copy(refresh_hbm, refresh_ref, local_sems.at[8]),
        pltpu.make_async_copy(grad_hbm.at[0], grad_ref, local_sems.at[0]),
    ]
    for copy in loads:
        copy.start()
    partners = greet(place)
    device = lax.axis_index("dp") * lax.axis_size("fsdp") + lax.axis_index("fsdp")
    loads[0].wait()
    loads[1].wait()
    packed, entry, live, fresh, ahead = index_tables(owner_ref[...], refresh_ref[...], device)
    table_vmem[0:1, :] = packed
    table_vmem[1:2, 0 : entry.shape[1]] = entry
    load_table = pltpu.make_async_copy(table_vmem, table, local_sems.at[6])
    load_table.start()
    pl.semaphore_wait(pltpu.get_barrier_semaphore(), partners)
    load_table.wait()
    loads[2].wait()

    def base(core, hop, part):
        slot, at, _, _ = PARTS[part]
        return ((core * PLANES + place.up(hop)) * CAP + slot) * COLS + at

    core_copies = {}
    plane_copies = {}

    def pack(part):
        slot, at, size, _ = PARTS[part]
        for h, hop in enumerate(CHUNKS):
            start = base(1 - place.core, hop, part)
            if part == SECOND:
                core_copies[AHEAD, h].wait_send()
                core_copies[BEHIND, h].wait_send()

            def one(e, carry, h=h, start=start):
                core_out[h, at + e] = grad_ref[table[0, start + e]]
                return carry

            lax.fori_loop(0, size, one, 0, unroll=4)
            span = pl.ds(at, size)
            core_copies[part, h] = remote(
                core_out.at[h, span], core_in.at[slot, h, span], core_s.at[part, h], core_r.at[part, h], place.sibling()
            )
            core_copies[part, h].start()

    def add(part):
        slot, at, size, _ = PARTS[part]
        for h, hop in enumerate(CHUNKS):
            core_copies[part, h].wait_recv()
            start = base(place.core, hop, part)

            def one(e, carry, h=h, hop=hop, start=start):
                total = grad_ref[table[0, start + e]] + core_in[slot, h, at + e]
                if hop:
                    plane_out[slot, h, at + e] = total.astype(BF16)
                else:
                    core_in[slot, h, at + e] = total
                return carry

            lax.fori_loop(0, size, one, 0, unroll=4)
            if hop:
                span = pl.ds(at, size)
                plane_copies[part, h] = remote(
                    plane_out.at[slot, h, span], plane_in.at[slot, h, span], plane_s.at[part, h], plane_r.at[part, h],
                    place.above(hop),
                )
                if part != SECOND:
                    plane_copies[part, h].start()

    def planes_send(part):
        for h in range(len(HOPS)):
            plane_copies[part, h].start()

    def col_copy(part, which, t):
        slot, at, _, share = PARTS[part]
        col, half = place.turn(t), place.half(which)
        return remote(
            col_out.at[slot, half, at + col // share], held.at[part, half, place.col],
            col_s.at[part, which, t], col_r.at[part, which, t], place.at(place.core, place.plane, col),
        )

    def fold(part, which):
        slot, at, size, share = PARTS[part]
        half = place.half(which)
        for h, hop in enumerate(HOPS):
            if (hop == 2) == (which == 1):
                plane_copies[part, h].wait_recv()

        def one(e, carry):
            if which == 0:
                total = plane_in[slot, 0, at + e].astype(F32) + plane_in[slot, 1, at + e].astype(F32)
            else:
                total = core_in[slot, len(HOPS), at + e] + plane_in[slot, 2, at + e].astype(F32)
            col_out[slot, half, at + e] = total.astype(BF16)
            return carry

        lax.fori_loop(0, size, one, 0, unroll=4)

        def send(i, carry):
            col_copy(part, which, spread_order(i)).start()
            return carry

        lax.fori_loop(1, COLS, send, 0)
        held[part, half, place.col] = col_out[slot, half, at + place.col // share]

    def col_wait(part):
        for which in range(2):

            def one(t, carry):
                col_copy(part, which, t).wait_recv()
                return carry

            lax.fori_loop(1, COLS, one, 0)

    def region(plane, slot):
        return ((place.core * PLANES + plane) * CAP + slot) * COLS

    def row_copy(which, t):
        col, half = place.turn(t), place.half(which)
        return remote(
            step.at[0, half, col], rows.at[half, place.col],
            row_s.at[which, t], row_r.at[which, t], place.at(place.core, place.plane, col),
        )

    def rows_send():
        for which in range(2):

            def one(i, carry):
                row_copy(which, spread_order(i)).start()
                return carry

            lax.fori_loop(1, COLS, one, 0)
        rows[:, place.col] = step[0, :, place.col]

    up_copies = {}

    def rows_up():
        for which in range(2):

            def one(t, carry):
                row_copy(which, t).wait_recv()
                return carry

            lax.fori_loop(1, COLS, one, 0)
            for h, hop in enumerate(HOPS):
                if (hop == 2) == (which == 1):
                    up_copies[h] = remote(
                        rows.at[place.half(which)], every.at[pl.ds(region(place.plane, 0), COLS)],
                        up_s.at[h], up_r.at[h], place.above(hop),
                    )
                    up_copies[h].start()
        every[pl.ds(region(place.plane, 0), COLS)] = rows[place.low]

    def back_copy(h, t):
        plane, col = place.up(CHUNKS[h]), place.turn(t)
        return remote(
            step.at[1, lax.rem(plane, 2), col], every.at[region(place.plane, 1) + place.col],
            back_s.at[h, t], back_r.at[h, t], place.at(place.core, plane, col),
        )

    def back_send():
        def far(i, carry):
            back_copy(2, spread_order(i)).start()
            return carry

        def near(i, carry):
            back_copy(0, spread_order(i)).start()
            back_copy(1, spread_order(i)).start()
            return carry

        def here(i, carry):
            back_copy(3, spread_order(i)).start()
            return carry

        lax.fori_loop(0, COLS, far, 0)
        lax.fori_loop(0, COLS, near, 0)
        lax.fori_loop(1, COLS, here, 0)
        every[region(place.plane, 1) + place.col] = step[1, place.low, place.col]

    def back_wait(h):
        def one(t, carry):
            back_copy(h, t).wait_recv()
            return carry

        lax.fori_loop(int(CHUNKS[h] == 0), COLS, one, 0)

    back_cores = {}

    def over(slot, h):
        here = every.at[pl.ds(region(place.up(PLANES - CHUNKS[h]), slot), COLS)]
        back_cores[slot, h] = remote(here, here, core_s2.at[slot, h], core_r2.at[slot, h], place.sibling())
        back_cores[slot, h].start()

    pack(AHEAD)
    pack(BEHIND)
    add(AHEAD)
    loads = []
    for i, (src, dst) in enumerate(
        ((stats_left, gram.at[0]), (stats_right, gram.at[1]), (roots_left, keep.at[0]), (roots_right, keep.at[1]),
         (params_hbm, result_ref))
    ):
        copy = pltpu.make_async_copy(src, dst, local_sems.at[1 + i])
        copy.start()
        loads.append(copy)
    add(BEHIND)
    pack(SECOND)
    fold(AHEAD, 0)
    fold(AHEAD, 1)
    add(SECOND)
    fold(BEHIND, 0)
    planes_send(SECOND)
    fold(BEHIND, 1)
    for copy in loads:
        copy.wait()

    def grad_of(part):
        return held[part].reshape(WIDTH, WIDTH)

    def first_grad():
        both = jnp.where(ahead, grad_of(AHEAD).astype(F32), grad_of(BEHIND).astype(F32))
        return both.astype(BF16)

    def put_step(slot, value):
        step[slot] = value.reshape(2, COLS, ROWS, WIDTH)

    def factor(side, slot, grad):
        fresh_part = dot_t(grad, grad, ((1,), (0,))[side])
        return beta_decay * gram[side, slot] + ((1.0 - beta_decay) / WIDTH) * fresh_part

    def factors(slot, grad):
        for side in range(2):
            gram[side, slot] = live[slot].astype(F32) * factor(side, slot, grad)

    def sweeps(count):
        def one(i, carry):
            root_sweep(inverse.at[0], mixed.at[0])
            root_sweep(inverse.at[1], mixed.at[1])
            return carry

        lax.fori_loop(0, count, one, 0)

    col_wait(AHEAD)
    for side in range(2):
        root_start(factor(side, 0, grad_of(AHEAD)), inverse.at[side], mixed.at[side])
    sweeps(1)
    col_wait(BEHIND)
    put_step(0, kept_step(keep[0, 0], first_grad(), keep[1, 0]))
    rows_send()
    sweeps(1)
    fold(SECOND, 0)
    fold(SECOND, 1)
    sweeps(1)
    rows_up()
    sweeps(2)
    col_wait(SECOND)
    put_step(1, kept_step(keep[0, 1], grad_of(SECOND), keep[1, 1]))
    grad = grad_of(AHEAD)
    inner = dot(inverse[0].astype(BF16), grad)
    renewed = scaled_step(dot(inner.astype(BF16), inverse[1].astype(BF16)), grad)
    late = step[1].reshape(WIDTH, WIDTH)
    put_step(1, jnp.where(fresh > 0, renewed.astype(F32), late.astype(F32)).astype(BF16))
    back_send()
    factors(0, first_grad())
    factors(1, grad_of(SECOND))
    over(0, 3)
    for h in range(len(HOPS)):
        up_copies[h].wait_recv()
        over(0, h)
    for h in range(PLANES):
        core_copies[SECOND, h].wait_send()
    for copy in plane_copies.values():
        copy.wait_send()
    for part in range(len(PARTS)):
        for which in range(2):

            def done(t, carry):
                col_copy(part, which, t).wait_send()
                return carry

            lax.fori_loop(1, COLS, done, 0)
    for which in range(2):

        def row_done(t, carry):
            row_copy(which, t).wait_send()
            return carry

        lax.fori_loop(1, COLS, row_done, 0)
    for copy in up_copies.values():
        copy.wait_send()
    for h in (2, 0, 1, 3):
        back_wait(h)
        over(1, h)
    for h in range(len(CHUNKS)):

        def back_done(t, carry):
            back_copy(h, t).wait_send()
            return carry

        lax.fori_loop(int(CHUNKS[h] == 0), COLS, back_done, 0)
    for copy in back_cores.values():
        copy.wait_recv()

    def apply(b, carry):
        change = every[table[1, b]].astype(F32)
        result_ref[b] = (result_ref[b].astype(F32) - change).astype(BF16)
        return carry

    lax.fori_loop(0, result_ref.shape[0], apply, 0, unroll=4)
    for copy in back_cores.values():
        copy.wait_send()


def store_kernel(result_ref, gram, out_params, out_left, out_right, sems):
    copies = [
        pltpu.make_async_copy(gram.at[0], out_left, sems.at[0]),
        pltpu.make_async_copy(gram.at[1], out_right, sems.at[1]),
        pltpu.make_async_copy(result_ref, out_params, sems.at[2]),
    ]
    for copy in copies:
        copy.start()
    for copy in copies:
        copy.wait()


VMEM = pl.BlockSpec(memory_space=pltpu.VMEM)
HBM = pl.BlockSpec(memory_space=pltpu.HBM)


def body(grad_partial, params, stats_left, stats_right, roots_left, roots_right, owner, refresh):
    count = params.shape[0]
    dma = pltpu.SemaphoreType.DMA
    hops = len(HOPS)
    piece = (COLS, ROWS, WIDTH)
    square = (WIDTH, WIDTH)
    result, gram = pl.pallas_call(
        whole_kernel,
        name="whole",
        out_shape=[pltpu.VMEM(params.shape, BF16), pltpu.VMEM((2, CAP) + square, F32)],
        in_specs=[HBM] * 8,
        out_specs=[VMEM] * 2,
        scratch_shapes=[
            pltpu.VMEM((1, count), jnp.int32),
            pltpu.VMEM((1, count), jnp.int32),
            pltpu.VMEM((8, SLOTS), jnp.int32),
            pltpu.SMEM((8, SLOTS), jnp.int32),
            pltpu.VMEM((count, ROWS, WIDTH), F32),
            pltpu.VMEM((2, CAP) + square, F32),
            pltpu.VMEM((2,) + square, F32),
            pltpu.VMEM((2,) + square, F32),
            pltpu.VMEM((PLANES,) + piece, F32),
            pltpu.VMEM((CAP, PLANES) + piece, F32),
            pltpu.VMEM((CAP, hops) + piece, BF16),
            pltpu.VMEM((CAP, hops) + piece, BF16),
            pltpu.VMEM((CAP, 2) + piece, BF16),
            pltpu.VMEM((len(PARTS), 2) + piece, BF16),
            pltpu.VMEM((CAP, 2) + piece, BF16),
            pltpu.VMEM((2,) + piece, BF16),
            pltpu.VMEM((SLOTS, ROWS, WIDTH), BF16),
            dma((9,)),
            dma((len(PARTS), PLANES)), dma((len(PARTS), PLANES)),
            dma((len(PARTS), hops)), dma((len(PARTS), hops)),
            dma((len(PARTS), 2, COLS)), dma((len(PARTS), 2, COLS)),
            dma((2, COLS)), dma((2, COLS)),
            dma((hops,)), dma((hops,)),
            dma((PLANES, COLS)), dma((PLANES, COLS)),
            dma((CAP, PLANES)), dma((CAP, PLANES)),
        ],
        compiler_params=pltpu.CompilerParams(collective_id=0, has_side_effects=True, vmem_limit_bytes=40 << 20),
    )(*[
        pltpu.with_memory_space_constraint(array, pltpu.HBM)
        for array in (
            owner.reshape(1, count), refresh.reshape(1, count),
            grad_partial, params, stats_left, stats_right, roots_left, roots_right,
        )
    ])
    return pl.pallas_call(
        store_kernel,
        name="store",
        out_shape=[
            jax.ShapeDtypeStruct(params.shape, BF16),
            jax.ShapeDtypeStruct((CAP,) + square, F32),
            jax.ShapeDtypeStruct((CAP,) + square, F32),
        ],
        in_specs=[VMEM] * 2,
        out_specs=[HBM] * 3,
        scratch_shapes=[dma((3,))],
        compiler_params=pltpu.CompilerParams(vmem_limit_bytes=1 << 20),
    )(
        pltpu.with_memory_space_constraint(result, pltpu.VMEM),
        pltpu.with_memory_space_constraint(gram, pltpu.VMEM),
    )


def solution(mesh):
    in_specs = (
        P("dp", None, "fsdp", None),
        P(None, "fsdp", None),
        P(("dp", "fsdp"), None, None),
        P(("dp", "fsdp"), None, None),
        P(("dp", "fsdp"), None, None),
        P(("dp", "fsdp"), None, None),
        P(),
        P(),
    )
    out_specs = (
        P(None, "fsdp", None),
        P(("dp", "fsdp"), None, None),
        P(("dp", "fsdp"), None, None),
    )
    return jax.shard_map(body, mesh=mesh, in_specs=in_specs, out_specs=out_specs, check_vma=False)
```

```python
import jax
import jax.numpy as jnp
from jax import lax
from jax.experimental import pallas as pl
from jax.experimental.pallas import tpu as pltpu
from jax.sharding import PartitionSpec as P

MESH = pl.DeviceIdType.MESH
F32 = jnp.float32
BF16 = jnp.bfloat16

beta_decay = 0.9
learn_rate = 0.2
epsilon = 1e-06
ITERS = 6

PLANES = 4
SIDE = 4
COLS = SIDE * SIDE
CORES = 2
CAP = 2
ROWS = 16
WIDTH = 512
SLOTS = CORES * PLANES * CAP * COLS
HOPS = (1, 3, 2)
CHUNKS = HOPS + (0,)
AHEAD, BEHIND, SECOND = range(3)
PARTS = ((0, 0, COLS // 2, 2), (0, COLS // 2, COLS // 2, 2), (1, 0, COLS, 1))


class Place:
    def __init__(self):
        dp = lax.axis_index("dp")
        fsdp = lax.axis_index("fsdp")
        self.core = lax.rem(dp, 2)
        self.plane = (dp // 2) * 2 + fsdp // COLS
        self.low = fsdp // COLS
        self.col = lax.rem(fsdp, COLS)

    def at(self, core, plane, col):
        return ((plane // 2) * 2 + core, lax.rem(plane, 2) * COLS + col)

    def sibling(self):
        return self.at(1 - self.core, self.plane, self.col)

    def up(self, hop):
        return lax.rem(self.plane + hop, PLANES)

    def above(self, hop):
        return self.at(self.core, self.up(hop), self.col)

    def turn(self, t):
        y, x = self.col // SIDE, lax.rem(self.col, SIDE)
        return lax.rem(y + t // SIDE, SIDE) * SIDE + lax.rem(x + lax.rem(t, SIDE), SIDE)

    def turned(self, t):
        y, x = self.col // SIDE, lax.rem(self.col, SIDE)
        return lax.rem(y + SIDE - t // SIDE, SIDE) * SIDE + lax.rem(x + SIDE - lax.rem(t, SIDE), SIDE)

    def half(self, which):
        return 1 - self.low if which == 0 else self.low


def greet(place):
    partners = [place.sibling()] + [place.above(hop) for hop in HOPS]
    partners += [place.at(place.core, place.plane, place.turn(t)) for t in range(1, COLS)]
    for partner in partners:
        pl.semaphore_signal(pltpu.get_barrier_semaphore(), inc=1, device_id=partner, device_id_type=MESH)
    return len(partners)


def spread_order(i):
    return lax.rem(5 * i, COLS)


def count_up(mask, axis):
    return jnp.sum(mask.astype(jnp.int32), axis=axis, keepdims=True)


def index_tables(owner, refresh, device):
    count = owner.shape[1]
    row = lax.broadcasted_iota(jnp.int32, (count, count), 0)
    column = lax.broadcasted_iota(jnp.int32, (count, count), 1)
    owner_down = jnp.sum(jnp.where(row == column, owner, 0), axis=1, keepdims=True)
    refresh_down = jnp.sum(jnp.where(row == column, refresh, 0), axis=1, keepdims=True)
    same = owner_down == owner
    other_down = count_up(((owner_down ^ 1) == owner) & (refresh > 0), 1)
    ahead_down = (refresh_down > 0) | (((owner_down & 1) == 0) & (other_down == 0))
    rank = count_up(same & (row < column), 0)
    rank_down = count_up(same & (column < row), 1)

    def first(own):
        core, plane = (own >> 5) & 1, 2 * (own >> 6) + ((own >> 4) & 1)
        return (core * PLANES + plane) * CAP * COLS

    entry = first(owner) + (rank + refresh) * COLS + (owner & (COLS - 1))
    col_down = owner_down & (COLS - 1)
    pair_down = (col_down >> 1) + jnp.where(ahead_down, 0, COLS // 2)
    place_down = first(owner_down) + jnp.where(rank_down > 0, COLS + col_down, pair_down)
    spot = lax.broadcasted_iota(jnp.int32, (count, SLOTS), 1)
    block = lax.broadcasted_iota(jnp.int32, (count, SLOTS), 0)
    packed = jnp.sum(jnp.where(place_down == spot, block, 0), axis=0, keepdims=True)
    mine = owner == device
    live = [count_up(mine & (rank == slot), 1) for slot in range(CAP)]
    fresh = count_up(mine & (refresh > 0), 1)
    other = count_up((owner == (device ^ 1)) & (refresh > 0), 1)
    ahead = (fresh > 0) | (((device & 1) == 0) & (other == 0))
    return jnp.minimum(packed, count - 1), jnp.minimum(entry, SLOTS - 1), live, fresh, ahead


def remote(src, dst, send, recv, device):
    return pltpu.make_async_remote_copy(
        src_ref=src, dst_ref=dst, send_sem=send, recv_sem=recv, device_id=device, device_id_type=MESH
    )


def dot(left, right):
    return jnp.dot(left, right, preferred_element_type=F32)


def dot_t(left, right, dims):
    return lax.dot_general(left, right, ((dims, dims), ((), ())), preferred_element_type=F32)


def halves(value):
    high = value.astype(BF16)
    return high, (value - high.astype(F32)).astype(BF16)


def total_square(value):
    return jnp.sum(value * value, axis=(0, 1), keepdims=True)


def root_start(factor, result, mixed, pair):
    scale = jnp.sqrt(total_square(factor) + epsilon)
    start = factor * (1.0 / scale)
    mixed[...] = start
    row = lax.broadcasted_iota(jnp.int32, start.shape, 0)
    column = lax.broadcasted_iota(jnp.int32, start.shape, 1)
    ident = jnp.where(row == column, 1.0, 0.0).astype(F32)
    first = lax.rsqrt(jnp.sqrt(scale)) * (1.25 * ident - 0.25 * start)
    result[...] = first
    pair[0:WIDTH] = start.astype(BF16)
    pair[WIDTH : 2 * WIDTH] = first.astype(BF16)


def root_sweep(results, mixeds, pairs, with_result):
    sides = range(len(results))
    lows = [pair[0:WIDTH] for pair in pairs]
    products = [dot(pairs[i][...] if with_result else lows[i], lows[i]) for i in sides]
    edges = [(products[i][0:WIDTH] - 10.0 * mixeds[i][...]) * (1.0 / 16.0) for i in sides]
    edge_lows = [edge.astype(BF16) for edge in edges]
    fourths = [dot(edge_lows[i], edge_lows[i]) + 3.125 * edges[i] for i in sides]
    if with_result:
        for i in sides:
            value = 1.25 * results[i][...] - 0.25 * products[i][WIDTH : 2 * WIDTH]
            results[i][...] = value
            pairs[i][WIDTH : 2 * WIDTH] = value.astype(BF16)
    for i in sides:
        value = (625.0 / 256.0) * mixeds[i][...] + dot(fourths[i].astype(BF16), lows[i])
        mixeds[i][...] = value
        pairs[i][0:WIDTH] = value.astype(BF16)


def root_end(result, pair):
    return 1.25 * result[...] - 0.25 * dot(pair[WIDTH : 2 * WIDTH], pair[0:WIDTH])


def scaled_step(precond, grad):
    ratio = jnp.sqrt(total_square(grad.astype(F32))) / jnp.sqrt(total_square(precond) + epsilon)
    return (learn_rate * precond * ratio).astype(BF16)


def kept_step(left, grad, right):
    inner = dot(left, grad)
    inner_high, inner_low = halves(inner[0:WIDTH] + inner[WIDTH : 2 * WIDTH])
    right_high, right_low = right[0:WIDTH], right[WIDTH : 2 * WIDTH]
    precond = dot(inner_high, right_high) + (dot(inner_low, right_high) + dot(inner_high, right_low))
    return scaled_step(precond, grad)


def whole_kernel(
    owner_hbm, refresh_hbm, grad_hbm, params_hbm, stats_left, stats_right, roots_left, roots_right,
    result_ref, gram,
    owner_ref, refresh_ref, table_vmem, table, grad_ref, keep, split, inverse, mixed, pair,
    core_out, core_in, plane_out, plane_in, col_out, held, step, rows, every,
    local_sems, core_s, core_r, plane_s, plane_r, col_s, col_r,
    row_s, row_r, up_s, up_r, back_s, back_r, core_s2, core_r2,
):
    place = Place()
    loads = [
        pltpu.make_async_copy(owner_hbm, owner_ref, local_sems.at[7]),
        pltpu.make_async_copy(refresh_hbm, refresh_ref, local_sems.at[8]),
        pltpu.make_async_copy(grad_hbm.at[0], grad_ref, local_sems.at[0]),
    ]
    for copy in loads:
        copy.start()
    partners = greet(place)
    device = lax.axis_index("dp") * lax.axis_size("fsdp") + lax.axis_index("fsdp")
    loads[0].wait()
    loads[1].wait()
    packed, entry, live, fresh, ahead = index_tables(owner_ref[...], refresh_ref[...], device)
    table_vmem[0:1, :] = packed
    table_vmem[1:2, 0 : entry.shape[1]] = entry
    load_table = pltpu.make_async_copy(table_vmem, table, local_sems.at[6])
    load_table.start()
    pl.semaphore_wait(pltpu.get_barrier_semaphore(), partners)
    load_table.wait()
    loads[2].wait()

    def base(core, hop, part):
        slot, at, _, _ = PARTS[part]
        return ((core * PLANES + place.up(hop)) * CAP + slot) * COLS + at

    core_copies = {}
    plane_copies = {}

    def pack(part):
        slot, at, size, _ = PARTS[part]
        for h, hop in enumerate(CHUNKS):
            start = base(1 - place.core, hop, part)
            if part == SECOND:
                core_copies[AHEAD, h].wait_send()
                core_copies[BEHIND, h].wait_send()

            def one(e, carry, h=h, start=start):
                core_out[h, at + e] = grad_ref[table[0, start + e]]
                return carry

            lax.fori_loop(0, size, one, 0, unroll=4)
            span = pl.ds(at, size)
            core_copies[part, h] = remote(
                core_out.at[h, span], core_in.at[slot, h, span], core_s.at[part, h], core_r.at[part, h], place.sibling()
            )
            core_copies[part, h].start()

    def add(part):
        slot, at, size, _ = PARTS[part]
        for h, hop in enumerate(CHUNKS):
            core_copies[part, h].wait_recv()
            start = base(place.core, hop, part)

            def one(e, carry, h=h, hop=hop, start=start):
                total = grad_ref[table[0, start + e]] + core_in[slot, h, at + e]
                if hop:
                    plane_out[slot, h, at + e] = total.astype(BF16)
                else:
                    core_in[slot, h, at + e] = total
                return carry

            lax.fori_loop(0, size, one, 0, unroll=4)
            if hop:
                span = pl.ds(at, size)
                plane_copies[part, h] = remote(
                    plane_out.at[slot, h, span], plane_in.at[slot, h, span], plane_s.at[part, h], plane_r.at[part, h],
                    place.above(hop),
                )
                if part != SECOND:
                    plane_copies[part, h].start()

    def planes_send(part):
        for h in range(len(HOPS)):
            plane_copies[part, h].start()

    def col_copy(part, which, t):
        slot, at, _, share = PARTS[part]
        col, half = place.turn(t), place.half(which)
        return remote(
            col_out.at[slot, half, at + col // share], held.at[part, half, place.col],
            col_s.at[part, which], col_r.at[part, which], place.at(place.core, place.plane, col),
        )

    def most(ref, send, recv):
        return remote(ref, ref, send, recv, place.sibling())

    def col_all(part, which):
        return most(held.at[part, place.half(which), pl.ds(0, COLS - 1)], col_s.at[part, which], col_r.at[part, which])

    def fold(part, which):
        slot, at, size, share = PARTS[part]
        half = place.half(which)
        for h, hop in enumerate(HOPS):
            if (hop == 2) == (which == 1):
                plane_copies[part, h].wait_recv()

        def one(e, carry):
            if which == 0:
                total = plane_in[slot, 0, at + e].astype(F32) + plane_in[slot, 1, at + e].astype(F32)
            else:
                total = core_in[slot, len(HOPS), at + e] + plane_in[slot, 2, at + e].astype(F32)
            col_out[slot, half, at + e] = total.astype(BF16)
            return carry

        lax.fori_loop(0, size, one, 0, unroll=4)

        def send(i, carry):
            col_copy(part, which, spread_order(i)).start()
            return carry

        lax.fori_loop(1, COLS, send, 0)
        held[part, half, place.col] = col_out[slot, half, at + place.col // share]

    def col_wait(part):
        for which in range(2):
            col_all(part, which).wait_recv()

    def region(plane, slot):
        return ((place.core * PLANES + plane) * CAP + slot) * COLS

    def row_copy(slot, t):
        col = place.turn(t)
        return remote(
            step.at[slot, 1 - place.low, col], rows.at[slot, place.col],
            row_s.at[slot], row_r.at[slot, t], place.at(place.core, place.plane, col),
        )

    def back_copy(slot, far, t):
        plane, col = place.up(2 * far), place.turn(t)
        return remote(
            step.at[slot, place.low, col], every.at[region(place.plane, slot) + place.col],
            back_s.at[slot, far], back_r.at[slot, far], place.at(place.core, plane, col),
        )

    def up_copy(slot, h, t):
        col = place.turned(t)
        return remote(
            rows.at[slot, col], every.at[region(place.plane, slot) + col],
            up_s.at[slot, h], up_r.at[slot, h], place.above(HOPS[h]),
        )

    def rows_send(slot):
        def one(i, carry):
            row_copy(slot, spread_order(i)).start()
            return carry

        lax.fori_loop(1, COLS, one, 0)
        rows[slot, place.col] = step[slot, 1 - place.low, place.col]

    def back_send(slot):
        def far(i, carry):
            back_copy(slot, 1, spread_order(i)).start()
            return carry

        def here(i, carry):
            back_copy(slot, 0, spread_order(i)).start()
            return carry

        lax.fori_loop(0, COLS, far, 0)
        lax.fori_loop(1, COLS, here, 0)
        every[region(place.plane, slot) + place.col] = step[slot, place.low, place.col]

    def back_up(slot):
        def up(t):
            for h in range(2):
                up_copy(slot, h, t).start()

        def one(i, carry):
            row_copy(slot, spread_order(i)).wait_recv()
            up(spread_order(i))
            return carry

        up(0)
        lax.fori_loop(1, COLS, one, 0)

    def piece(count):
        return every.at[pl.ds(0, count)]

    def row_all(slot):
        return most(rows.at[slot, pl.ds(0, COLS - 1)], row_s.at[slot], row_r.at[slot, 0])

    def back_all(slot, far):
        return most(piece(COLS - 1 + far), back_s.at[slot, far], back_r.at[slot, far])

    def up_all(slot, h):
        return most(piece(COLS), up_s.at[slot, h], up_r.at[slot, h])

    def back_over(slot):
        for h in (3, 2, 0, 1):
            if h < 2:
                up_all(slot, h).wait_recv()
            else:
                back_all(slot, 3 - h).wait_recv()
            over(slot, h)

    def back_sent(slot):
        row_all(slot).wait_send()
        for h in range(2):
            back_all(slot, h).wait_send()
            up_all(slot, h).wait_send()

    back_cores = {}

    def over(slot, h):
        here = every.at[pl.ds(region(place.up(PLANES - CHUNKS[h]), slot), COLS)]
        back_cores[slot, h] = remote(here, here, core_s2.at[slot, h], core_r2.at[slot, h], place.sibling())
        back_cores[slot, h].start()

    pack(AHEAD)
    pack(BEHIND)
    add(AHEAD)
    loads = []
    for i, (src, dst) in enumerate(
        ((stats_left, gram.at[0]), (stats_right, gram.at[1]), (roots_left, keep.at[0]), (roots_right, keep.at[1]),
         (params_hbm, result_ref))
    ):
        copy = pltpu.make_async_copy(src, dst, local_sems.at[1 + i])
        copy.start()
        loads.append(copy)
    add(BEHIND)
    pack(SECOND)
    fold(AHEAD, 0)
    fold(AHEAD, 1)
    add(SECOND)
    fold(BEHIND, 0)
    planes_send(SECOND)
    fold(BEHIND, 1)
    for copy in loads:
        copy.wait()

    def grad_of(part):
        return held[part].reshape(WIDTH, WIDTH)

    def first_grad():
        both = jnp.where(ahead, grad_of(AHEAD).astype(F32), grad_of(BEHIND).astype(F32))
        return both.astype(BF16)

    def put_step(slot, value):
        step[slot] = value.reshape(2, COLS, ROWS, WIDTH)

    def factor(side, slot, grad):
        fresh_part = dot_t(grad, grad, ((1,), (0,))[side])
        return beta_decay * gram[side, slot] + ((1.0 - beta_decay) / WIDTH) * fresh_part

    def factors(slot, grad):
        for side in range(2):
            gram[side, slot] = live[slot].astype(F32) * factor(side, slot, grad)

    def sweep(with_result):
        root_sweep(
            [inverse.at[0], inverse.at[1]], [mixed.at[0], mixed.at[1]], [pair.at[0], pair.at[1]], with_result
        )

    def sweeps(count):
        def one(i, carry):
            sweep(True)
            return carry

        lax.fori_loop(0, count, one, 0)

    for side in range(2):
        for slot in range(CAP):
            high, low = halves(keep[side, slot])
            split[side, slot, 0:WIDTH] = high
            split[side, slot, WIDTH : 2 * WIDTH] = low
    col_wait(AHEAD)
    for side in range(2):
        root_start(factor(side, 0, grad_of(AHEAD)), inverse.at[side], mixed.at[side], pair.at[side])
    sweep(False)
    sweep(True)
    col_wait(BEHIND)
    put_step(0, kept_step(split[0, 0], first_grad(), split[1, 0]))
    rows_send(0)
    fold(SECOND, 0)
    fold(SECOND, 1)
    back_send(0)
    sweeps(1)
    back_up(0)
    sweeps(2)
    col_wait(SECOND)
    put_step(1, kept_step(split[0, 1], grad_of(SECOND), split[1, 1]))
    grad = grad_of(AHEAD)
    root_left, root_right = [root_end(inverse.at[side], pair.at[side]).astype(BF16) for side in range(2)]
    renewed = scaled_step(dot(dot(root_left, grad).astype(BF16), root_right), grad)
    late = step[1].reshape(WIDTH, WIDTH)
    put_step(1, jnp.where(fresh > 0, renewed.astype(F32), late.astype(F32)).astype(BF16))
    rows_send(1)
    back_send(1)
    back_up(1)
    back_over(0)
    factors(0, first_grad())
    factors(1, grad_of(SECOND))
    for h in range(PLANES):
        core_copies[SECOND, h].wait_send()
    for copy in plane_copies.values():
        copy.wait_send()
    for part in range(len(PARTS)):
        for which in range(2):
            col_all(part, which).wait_send()
    back_sent(0)
    back_over(1)
    back_sent(1)
    for copy in back_cores.values():
        copy.wait_recv()

    def apply(b, carry):
        change = every[table[1, b]].astype(F32)
        result_ref[b] = (result_ref[b].astype(F32) - change).astype(BF16)
        return carry

    lax.fori_loop(0, result_ref.shape[0], apply, 0, unroll=4)
    for copy in back_cores.values():
        copy.wait_send()


def store_kernel(result_ref, gram, out_params, out_left, out_right, sems):
    copies = [
        pltpu.make_async_copy(gram.at[0], out_left, sems.at[0]),
        pltpu.make_async_copy(gram.at[1], out_right, sems.at[1]),
        pltpu.make_async_copy(result_ref, out_params, sems.at[2]),
    ]
    for copy in copies:
        copy.start()
    for copy in copies:
        copy.wait()


VMEM = pl.BlockSpec(memory_space=pltpu.VMEM)
HBM = pl.BlockSpec(memory_space=pltpu.HBM)


def body(grad_partial, params, stats_left, stats_right, roots_left, roots_right, owner, refresh):
    count = params.shape[0]
    dma = pltpu.SemaphoreType.DMA
    hops = len(HOPS)
    piece = (COLS, ROWS, WIDTH)
    square = (WIDTH, WIDTH)
    result, gram = pl.pallas_call(
        whole_kernel,
        name="whole",
        out_shape=[pltpu.VMEM(params.shape, BF16), pltpu.VMEM((2, CAP) + square, F32)],
        in_specs=[HBM] * 8,
        out_specs=[VMEM] * 2,
        scratch_shapes=[
            pltpu.VMEM((1, count), jnp.int32),
            pltpu.VMEM((1, count), jnp.int32),
            pltpu.VMEM((8, SLOTS), jnp.int32),
            pltpu.SMEM((8, SLOTS), jnp.int32),
            pltpu.VMEM((count, ROWS, WIDTH), F32),
            pltpu.VMEM((2, CAP) + square, F32),
            pltpu.VMEM((2, CAP, 2 * WIDTH, WIDTH), BF16),
            pltpu.VMEM((2,) + square, F32),
            pltpu.VMEM((2,) + square, F32),
            pltpu.VMEM((2, 2 * WIDTH, WIDTH), BF16),
            pltpu.VMEM((PLANES,) + piece, F32),
            pltpu.VMEM((CAP, PLANES) + piece, F32),
            pltpu.VMEM((CAP, hops) + piece, BF16),
            pltpu.VMEM((CAP, hops) + piece, BF16),
            pltpu.VMEM((CAP, 2) + piece, BF16),
            pltpu.VMEM((len(PARTS), 2) + piece, BF16),
            pltpu.VMEM((CAP, 2) + piece, BF16),
            pltpu.VMEM((CAP,) + piece, BF16),
            pltpu.VMEM((SLOTS, ROWS, WIDTH), BF16),
            dma((9,)),
            dma((len(PARTS), PLANES)), dma((len(PARTS), PLANES)),
            dma((len(PARTS), hops)), dma((len(PARTS), hops)),
            dma((len(PARTS), 2)), dma((len(PARTS), 2)),
            dma((CAP,)), dma((CAP, COLS)),
            dma((CAP, 2)), dma((CAP, 2)),
            dma((CAP, 2)), dma((CAP, 2)),
            dma((CAP, PLANES)), dma((CAP, PLANES)),
        ],
        compiler_params=pltpu.CompilerParams(collective_id=0, has_side_effects=True, vmem_limit_bytes=46 << 20),
    )(*[
        pltpu.with_memory_space_constraint(array, pltpu.HBM)
        for array in (
            owner.reshape(1, count), refresh.reshape(1, count),
            grad_partial, params, stats_left, stats_right, roots_left, roots_right,
        )
    ])
    return pl.pallas_call(
        store_kernel,
        name="store",
        out_shape=[
            jax.ShapeDtypeStruct(params.shape, BF16),
            jax.ShapeDtypeStruct((CAP,) + square, F32),
            jax.ShapeDtypeStruct((CAP,) + square, F32),
        ],
        in_specs=[VMEM] * 2,
        out_specs=[HBM] * 3,
        scratch_shapes=[dma((3,))],
        compiler_params=pltpu.CompilerParams(vmem_limit_bytes=1 << 20),
    )(
        pltpu.with_memory_space_constraint(result, pltpu.VMEM),
        pltpu.with_memory_space_constraint(gram, pltpu.VMEM),
    )


def solution(mesh):
    in_specs = (
        P("dp", None, "fsdp", None),
        P(None, "fsdp", None),
        P(("dp", "fsdp"), None, None),
        P(("dp", "fsdp"), None, None),
        P(("dp", "fsdp"), None, None),
        P(("dp", "fsdp"), None, None),
        P(),
        P(),
    )
    out_specs = (
        P(None, "fsdp", None),
        P(("dp", "fsdp"), None, None),
        P(("dp", "fsdp"), None, None),
    )
    return jax.shard_map(body, mesh=mesh, in_specs=in_specs, out_specs=out_specs, check_vma=False)
```

```python
import jax
import jax.numpy as jnp
from jax import lax
from jax.experimental import pallas as pl
from jax.experimental.pallas import tpu as pltpu
from jax.sharding import PartitionSpec as P

MESH = pl.DeviceIdType.MESH
F32 = jnp.float32
BF16 = jnp.bfloat16

beta_decay = 0.9
learn_rate = 0.2
epsilon = 1e-06
ITERS = 6

PLANES = 4
SIDE = 4
COLS = SIDE * SIDE
CORES = 2
CAP = 2
ROWS = 16
WIDTH = 512
SLOTS = CORES * PLANES * CAP * COLS
HOPS = (1, 3, 2)
CHUNKS = HOPS + (0,)
AHEAD, BEHIND, SECOND = range(3)
PARTS = ((0, 0, COLS // 2, 2), (0, COLS // 2, COLS // 2, 2), (1, 0, COLS, 1))


class Place:
    def __init__(self):
        dp = lax.axis_index("dp")
        fsdp = lax.axis_index("fsdp")
        self.core = lax.rem(dp, 2)
        self.plane = (dp // 2) * 2 + fsdp // COLS
        self.low = fsdp // COLS
        self.col = lax.rem(fsdp, COLS)

    def at(self, core, plane, col):
        return ((plane // 2) * 2 + core, lax.rem(plane, 2) * COLS + col)

    def sibling(self):
        return self.at(1 - self.core, self.plane, self.col)

    def up(self, hop):
        return lax.rem(self.plane + hop, PLANES)

    def above(self, hop):
        return self.at(self.core, self.up(hop), self.col)

    def turn(self, t):
        y, x = self.col // SIDE, lax.rem(self.col, SIDE)
        return lax.rem(y + t // SIDE, SIDE) * SIDE + lax.rem(x + lax.rem(t, SIDE), SIDE)

    def turned(self, t):
        y, x = self.col // SIDE, lax.rem(self.col, SIDE)
        return lax.rem(y + SIDE - t // SIDE, SIDE) * SIDE + lax.rem(x + SIDE - lax.rem(t, SIDE), SIDE)

    def half(self, which):
        return 1 - self.low if which == 0 else self.low


def greet(place):
    partners = [place.sibling()] + [place.above(hop) for hop in HOPS]
    partners += [place.at(place.core, place.plane, place.turn(t)) for t in range(1, COLS)]
    for partner in partners:
        pl.semaphore_signal(pltpu.get_barrier_semaphore(), inc=1, device_id=partner, device_id_type=MESH)
    return len(partners)


def spread_order(i):
    return lax.rem(5 * i, COLS)


def count_up(mask, axis):
    return jnp.sum(mask.astype(jnp.int32), axis=axis, keepdims=True)


def index_tables(owner, refresh, device):
    count = owner.shape[1]
    row = lax.broadcasted_iota(jnp.int32, (count, count), 0)
    column = lax.broadcasted_iota(jnp.int32, (count, count), 1)
    owner_down = jnp.sum(jnp.where(row == column, owner, 0), axis=1, keepdims=True)
    refresh_down = jnp.sum(jnp.where(row == column, refresh, 0), axis=1, keepdims=True)
    same = owner_down == owner
    other_down = count_up(((owner_down ^ 1) == owner) & (refresh > 0), 1)
    ahead_down = (refresh_down > 0) | (((owner_down & 1) == 0) & (other_down == 0))
    rank = count_up(same & (row < column), 0)
    rank_down = count_up(same & (column < row), 1)

    def first(own):
        core, plane = (own >> 5) & 1, 2 * (own >> 6) + ((own >> 4) & 1)
        return (core * PLANES + plane) * CAP * COLS

    entry = first(owner) + (rank + refresh) * COLS + (owner & (COLS - 1))
    col_down = owner_down & (COLS - 1)
    pair_down = (col_down >> 1) + jnp.where(ahead_down, 0, COLS // 2)
    place_down = first(owner_down) + jnp.where(rank_down > 0, COLS + col_down, pair_down)
    spot = lax.broadcasted_iota(jnp.int32, (count, SLOTS), 1)
    block = lax.broadcasted_iota(jnp.int32, (count, SLOTS), 0)
    packed = jnp.sum(jnp.where(place_down == spot, block, 0), axis=0, keepdims=True)
    mine = owner == device
    live = [count_up(mine & (rank == slot), 1) for slot in range(CAP)]
    fresh = count_up(mine & (refresh > 0), 1)
    other = count_up((owner == (device ^ 1)) & (refresh > 0), 1)
    ahead = (fresh > 0) | (((device & 1) == 0) & (other == 0))
    return jnp.minimum(packed, count - 1), jnp.minimum(entry, SLOTS - 1), live, fresh, ahead


def remote(src, dst, send, recv, device):
    return pltpu.make_async_remote_copy(
        src_ref=src, dst_ref=dst, send_sem=send, recv_sem=recv, device_id=device, device_id_type=MESH
    )


def dot(left, right):
    return jnp.dot(left, right, preferred_element_type=F32)


def dot_t(left, right, dims):
    return lax.dot_general(left, right, ((dims, dims), ((), ())), preferred_element_type=F32)


def halves(value):
    high = value.astype(BF16)
    return high, (value - high.astype(F32)).astype(BF16)


def total_square(value):
    return jnp.sum(value * value, axis=(0, 1), keepdims=True)


def root_start(factor, result, mixed, pair):
    scale = jnp.sqrt(total_square(factor) + epsilon)
    start = factor * (1.0 / scale)
    mixed[...] = start
    row = lax.broadcasted_iota(jnp.int32, start.shape, 0)
    column = lax.broadcasted_iota(jnp.int32, start.shape, 1)
    ident = jnp.where(row == column, 1.0, 0.0).astype(F32)
    first = lax.rsqrt(jnp.sqrt(scale)) * (1.25 * ident - 0.25 * start)
    result[...] = first
    pair[0:WIDTH] = start.astype(BF16)
    pair[WIDTH : 2 * WIDTH] = first.astype(BF16)


def root_sweep(results, mixeds, pairs, with_result):
    sides = range(len(results))
    lows = [pair[0:WIDTH] for pair in pairs]
    products = [dot(pairs[i][...] if with_result else lows[i], lows[i]) for i in sides]
    edges = [(products[i][0:WIDTH] - 10.0 * mixeds[i][...]) * (1.0 / 16.0) for i in sides]
    edge_lows = [edge.astype(BF16) for edge in edges]
    fourths = [dot(edge_lows[i], edge_lows[i]) + 3.125 * edges[i] for i in sides]
    if with_result:
        for i in sides:
            value = 1.25 * results[i][...] - 0.25 * products[i][WIDTH : 2 * WIDTH]
            results[i][...] = value
            pairs[i][WIDTH : 2 * WIDTH] = value.astype(BF16)
    for i in sides:
        value = (625.0 / 256.0) * mixeds[i][...] + dot(fourths[i].astype(BF16), lows[i])
        mixeds[i][...] = value
        pairs[i][0:WIDTH] = value.astype(BF16)


def root_end(result, pair):
    return 1.25 * result[...] - 0.25 * dot(pair[WIDTH : 2 * WIDTH], pair[0:WIDTH])


def scaled_step(precond, grad):
    ratio = jnp.sqrt(total_square(grad.astype(F32))) / jnp.sqrt(total_square(precond) + epsilon)
    return (learn_rate * precond * ratio).astype(BF16)


def kept_step(left, grad, right):
    inner = dot(left, grad)
    inner_high, inner_low = halves(inner[0:WIDTH] + inner[WIDTH : 2 * WIDTH])
    right_high, right_low = right[0:WIDTH], right[WIDTH : 2 * WIDTH]
    precond = dot(inner_high, right_high) + (dot(inner_low, right_high) + dot(inner_high, right_low))
    return scaled_step(precond, grad)


def whole_kernel(
    owner_hbm, refresh_hbm, grad_hbm, params_hbm, stats_left, stats_right, roots_left, roots_right,
    result_ref, gram,
    owner_ref, refresh_ref, table_vmem, table, grad_ref, keep, split, inverse, mixed, pair,
    core_out, core_in, plane_out, plane_in, col_out, held, step, rows, every,
    local_sems, core_s, core_r, plane_s, plane_r, col_s, col_r,
    row_s, row_r, up_s, up_r, back_s, back_r, core_s2, core_r2,
):
    place = Place()
    loads = [
        pltpu.make_async_copy(owner_hbm, owner_ref, local_sems.at[7]),
        pltpu.make_async_copy(refresh_hbm, refresh_ref, local_sems.at[8]),
        pltpu.make_async_copy(grad_hbm.at[0], grad_ref, local_sems.at[0]),
    ]
    for copy in loads:
        copy.start()
    partners = greet(place)
    device = lax.axis_index("dp") * lax.axis_size("fsdp") + lax.axis_index("fsdp")
    loads[0].wait()
    loads[1].wait()
    packed, entry, live, fresh, ahead = index_tables(owner_ref[...], refresh_ref[...], device)
    table_vmem[0:1, :] = packed
    table_vmem[1:2, 0 : entry.shape[1]] = entry
    load_table = pltpu.make_async_copy(table_vmem, table, local_sems.at[6])
    load_table.start()
    pl.semaphore_wait(pltpu.get_barrier_semaphore(), partners)
    load_table.wait()
    loads[2].wait()

    def base(core, hop, part):
        slot, at, _, _ = PARTS[part]
        return ((core * PLANES + place.up(hop)) * CAP + slot) * COLS + at

    core_copies = {}
    plane_copies = {}

    def most(ref, send, recv):
        return remote(ref, ref, send, recv, place.sibling())

    def core_sent(part):
        _, at, size, _ = PARTS[part]
        most(core_out.at[:, pl.ds(at, size)], core_s.at[part], core_r.at[part, 0]).wait_send()

    def plane_sent(part):
        slot, at, size, _ = PARTS[part]
        most(plane_out.at[slot, :, pl.ds(at, size)], plane_s.at[part], plane_r.at[part, 0]).wait_send()

    def pack(part):
        slot, at, size, _ = PARTS[part]
        for h, hop in enumerate(CHUNKS):
            start = base(1 - place.core, hop, part)
            if part == SECOND and h == 0:
                core_sent(AHEAD)
                core_sent(BEHIND)

            def one(e, carry, h=h, start=start):
                core_out[h, at + e] = grad_ref[table[0, start + e]]
                return carry

            lax.fori_loop(0, size, one, 0, unroll=4)
            span = pl.ds(at, size)
            core_copies[part, h] = remote(
                core_out.at[h, span], core_in.at[slot, h, span], core_s.at[part], core_r.at[part, h], place.sibling()
            )
            core_copies[part, h].start()

    def add(part):
        slot, at, size, _ = PARTS[part]
        for h, hop in enumerate(CHUNKS):
            core_copies[part, h].wait_recv()
            start = base(place.core, hop, part)

            def one(e, carry, h=h, hop=hop, start=start):
                total = grad_ref[table[0, start + e]] + core_in[slot, h, at + e]
                if hop:
                    plane_out[slot, h, at + e] = total.astype(BF16)
                else:
                    core_in[slot, h, at + e] = total
                return carry

            lax.fori_loop(0, size, one, 0, unroll=4)
            if hop:
                span = pl.ds(at, size)
                plane_copies[part, h] = remote(
                    plane_out.at[slot, h, span], plane_in.at[slot, h, span], plane_s.at[part], plane_r.at[part, h],
                    place.above(hop),
                )
                if part != SECOND:
                    plane_copies[part, h].start()

    def planes_send(part):
        for h in range(len(HOPS)):
            plane_copies[part, h].start()

    def col_copy(part, which, t):
        slot, at, _, share = PARTS[part]
        col, half = place.turn(t), place.half(which)
        return remote(
            col_out.at[slot, half, at + col // share], held.at[part, half, place.col],
            col_s.at[part, which], col_r.at[part, which], place.at(place.core, place.plane, col),
        )

    def col_all(part, which):
        return most(held.at[part, place.half(which), pl.ds(0, COLS - 1)], col_s.at[part, which], col_r.at[part, which])

    def fold(part, which):
        slot, at, size, share = PARTS[part]
        half = place.half(which)
        for h, hop in enumerate(HOPS):
            if (hop == 2) == (which == 1):
                plane_copies[part, h].wait_recv()

        def one(e, carry):
            if which == 0:
                total = plane_in[slot, 0, at + e].astype(F32) + plane_in[slot, 1, at + e].astype(F32)
            else:
                total = core_in[slot, len(HOPS), at + e] + plane_in[slot, 2, at + e].astype(F32)
            col_out[slot, half, at + e] = total.astype(BF16)
            return carry

        lax.fori_loop(0, size, one, 0, unroll=4)

        def send(i, carry):
            col_copy(part, which, spread_order(i)).start()
            return carry

        lax.fori_loop(1, COLS, send, 0)
        held[part, half, place.col] = col_out[slot, half, at + place.col // share]

    def col_wait(part):
        for which in range(2):
            col_all(part, which).wait_recv()

    def region(plane, slot):
        return ((place.core * PLANES + plane) * CAP + slot) * COLS

    def row_copy(slot, t):
        col = place.turn(t)
        return remote(
            step.at[slot, 1 - place.low, col], rows.at[slot, place.col],
            row_s.at[slot], row_r.at[slot, t], place.at(place.core, place.plane, col),
        )

    def back_copy(slot, far, t):
        plane, col = place.up(2 * far), place.turn(t)
        return remote(
            step.at[slot, place.low, col], every.at[region(place.plane, slot) + place.col],
            back_s.at[slot], back_r.at[slot, far], place.at(place.core, plane, col),
        )

    def up_copy(slot, h, t):
        col = place.turned(t)
        return remote(
            rows.at[slot, col], every.at[region(place.plane, slot) + col],
            up_s.at[slot], up_r.at[slot, h], place.above(HOPS[h]),
        )

    def rows_send(slot):
        def one(i, carry):
            row_copy(slot, spread_order(i)).start()
            return carry

        lax.fori_loop(1, COLS, one, 0)
        rows[slot, place.col] = step[slot, 1 - place.low, place.col]

    def back_send(slot):
        def far(i, carry):
            back_copy(slot, 1, spread_order(i)).start()
            return carry

        def here(i, carry):
            back_copy(slot, 0, spread_order(i)).start()
            return carry

        lax.fori_loop(0, COLS, far, 0)
        lax.fori_loop(1, COLS, here, 0)
        every[region(place.plane, slot) + place.col] = step[slot, place.low, place.col]

    def back_up(slot):
        def up(t):
            for h in range(2):
                up_copy(slot, h, t).start()

        def one(i, carry):
            row_copy(slot, spread_order(i)).wait_recv()
            up(spread_order(i))
            return carry

        up(0)
        lax.fori_loop(1, COLS, one, 0)

    def piece(count):
        return every.at[pl.ds(0, count)]

    def row_all(slot):
        return most(rows.at[slot, pl.ds(0, COLS - 1)], row_s.at[slot], row_r.at[slot, 0])

    def back_all(slot, far):
        return most(piece(COLS - 1 + far), back_s.at[slot], back_r.at[slot, far])

    def up_all(slot, h):
        return most(piece(COLS), up_s.at[slot], up_r.at[slot, h])

    def back_over(slot):
        for h in (3, 2, 0, 1):
            if h < 2:
                up_all(slot, h).wait_recv()
            else:
                back_all(slot, 3 - h).wait_recv()
            over(slot, h)

    def back_sent(slot):
        row_all(slot).wait_send()
        most(piece(2 * COLS - 1), back_s.at[slot], back_r.at[slot, 0]).wait_send()
        most(piece(2 * COLS), up_s.at[slot], up_r.at[slot, 0]).wait_send()

    core_all = most(piece(SLOTS // 2), core_s2.at[0], core_r2.at[0])

    def over(slot, h):
        here = every.at[pl.ds(region(place.up(PLANES - CHUNKS[h]), slot), COLS)]
        remote(here, here, core_s2.at[0], core_r2.at[0], place.sibling()).start()

    pack(AHEAD)
    pack(BEHIND)
    add(AHEAD)
    loads = []
    for i, (src, dst) in enumerate(
        ((roots_left, keep.at[0]), (roots_right, keep.at[1]), (stats_left, gram.at[0]), (stats_right, gram.at[1]),
         (params_hbm, result_ref))
    ):
        copy = pltpu.make_async_copy(src, dst, local_sems.at[1 + i])
        copy.start()
        loads.append(copy)
    add(BEHIND)
    pack(SECOND)
    for copy in loads[:2]:
        copy.wait()
    for side in range(2):
        for slot in range(CAP):
            high, low = halves(keep[side, slot])
            split[side, slot, 0:WIDTH] = high
            split[side, slot, WIDTH : 2 * WIDTH] = low
    fold(AHEAD, 0)
    fold(AHEAD, 1)
    add(SECOND)
    fold(BEHIND, 0)
    planes_send(SECOND)
    fold(BEHIND, 1)
    for copy in loads[2:]:
        copy.wait()

    def grad_of(part):
        return held[part].reshape(WIDTH, WIDTH)

    def first_grad():
        both = jnp.where(ahead, grad_of(AHEAD).astype(F32), grad_of(BEHIND).astype(F32))
        return both.astype(BF16)

    def put_step(slot, value):
        step[slot] = value.reshape(2, COLS, ROWS, WIDTH)

    def factor(side, slot, grad):
        fresh_part = dot_t(grad, grad, ((1,), (0,))[side])
        return beta_decay * gram[side, slot] + ((1.0 - beta_decay) / WIDTH) * fresh_part

    def factors(slot, grad):
        for side in range(2):
            gram[side, slot] = live[slot].astype(F32) * factor(side, slot, grad)

    def sweep(with_result):
        root_sweep(
            [inverse.at[0], inverse.at[1]], [mixed.at[0], mixed.at[1]], [pair.at[0], pair.at[1]], with_result
        )

    def sweeps(count):
        def one(i, carry):
            sweep(True)
            return carry

        lax.fori_loop(0, count, one, 0)

    col_wait(AHEAD)
    for side in range(2):
        root_start(factor(side, 0, grad_of(AHEAD)), inverse.at[side], mixed.at[side], pair.at[side])
    sweep(False)
    sweep(True)
    col_wait(BEHIND)
    put_step(0, kept_step(split[0, 0], first_grad(), split[1, 0]))
    rows_send(0)
    fold(SECOND, 0)
    fold(SECOND, 1)
    back_send(0)
    sweeps(1)
    back_up(0)
    sweeps(2)
    col_wait(SECOND)
    put_step(1, kept_step(split[0, 1], grad_of(SECOND), split[1, 1]))
    grad = grad_of(AHEAD)
    root_left, root_right = [root_end(inverse.at[side], pair.at[side]).astype(BF16) for side in range(2)]
    renewed = scaled_step(dot(dot(root_left, grad).astype(BF16), root_right), grad)
    late = step[1].reshape(WIDTH, WIDTH)
    put_step(1, jnp.where(fresh > 0, renewed.astype(F32), late.astype(F32)).astype(BF16))
    rows_send(1)
    back_send(1)
    back_up(1)
    back_over(0)
    factors(0, first_grad())
    factors(1, grad_of(SECOND))
    core_sent(SECOND)
    for part in range(len(PARTS)):
        plane_sent(part)
    for part in range(len(PARTS)):
        for which in range(2):
            col_all(part, which).wait_send()
    back_sent(0)
    back_over(1)
    back_sent(1)
    core_all.wait_recv()

    def apply(b, carry):
        change = every[table[1, b]].astype(F32)
        result_ref[b] = (result_ref[b].astype(F32) - change).astype(BF16)
        return carry

    lax.fori_loop(0, result_ref.shape[0], apply, 0, unroll=4)
    core_all.wait_send()


def store_kernel(result_ref, gram, out_params, out_left, out_right, sems):
    copies = []
    for slot in range(CAP):
        copies.append((gram.at[0, slot], out_left.at[slot]))
        copies.append((gram.at[1, slot], out_right.at[slot]))
    half = result_ref.shape[0] // 2
    for part in range(2):
        span = pl.ds(part * half, half)
        copies.append((result_ref.at[span], out_params.at[span]))
    copies = [pltpu.make_async_copy(src, dst, sems.at[i]) for i, (src, dst) in enumerate(copies)]
    for copy in copies:
        copy.start()
    for copy in copies:
        copy.wait()


VMEM = pl.BlockSpec(memory_space=pltpu.VMEM)
HBM = pl.BlockSpec(memory_space=pltpu.HBM)


def body(grad_partial, params, stats_left, stats_right, roots_left, roots_right, owner, refresh):
    count = params.shape[0]
    dma = pltpu.SemaphoreType.DMA
    hops = len(HOPS)
    piece = (COLS, ROWS, WIDTH)
    square = (WIDTH, WIDTH)
    result, gram = pl.pallas_call(
        whole_kernel,
        name="whole",
        out_shape=[pltpu.VMEM(params.shape, BF16), pltpu.VMEM((2, CAP) + square, F32)],
        in_specs=[HBM] * 8,
        out_specs=[VMEM] * 2,
        scratch_shapes=[
            pltpu.VMEM((1, count), jnp.int32),
            pltpu.VMEM((1, count), jnp.int32),
            pltpu.VMEM((8, SLOTS), jnp.int32),
            pltpu.SMEM((8, SLOTS), jnp.int32),
            pltpu.VMEM((count, ROWS, WIDTH), F32),
            pltpu.VMEM((2, CAP) + square, F32),
            pltpu.VMEM((2, CAP, 2 * WIDTH, WIDTH), BF16),
            pltpu.VMEM((2,) + square, F32),
            pltpu.VMEM((2,) + square, F32),
            pltpu.VMEM((2, 2 * WIDTH, WIDTH), BF16),
            pltpu.VMEM((PLANES,) + piece, F32),
            pltpu.VMEM((CAP, PLANES) + piece, F32),
            pltpu.VMEM((CAP, hops) + piece, BF16),
            pltpu.VMEM((CAP, hops) + piece, BF16),
            pltpu.VMEM((CAP, 2) + piece, BF16),
            pltpu.VMEM((len(PARTS), 2) + piece, BF16),
            pltpu.VMEM((CAP, 2) + piece, BF16),
            pltpu.VMEM((CAP,) + piece, BF16),
            pltpu.VMEM((SLOTS, ROWS, WIDTH), BF16),
            dma((9,)),
            dma((len(PARTS),)), dma((len(PARTS), PLANES)),
            dma((len(PARTS),)), dma((len(PARTS), hops)),
            dma((len(PARTS), 2)), dma((len(PARTS), 2)),
            dma((CAP,)), dma((CAP, COLS)),
            dma((CAP,)), dma((CAP, 2)),
            dma((CAP,)), dma((CAP, 2)),
            dma((1,)), dma((1,)),
        ],
        compiler_params=pltpu.CompilerParams(collective_id=0, has_side_effects=True, vmem_limit_bytes=46 << 20),
    )(*[
        pltpu.with_memory_space_constraint(array, pltpu.HBM)
        for array in (
            owner.reshape(1, count), refresh.reshape(1, count),
            grad_partial, params, stats_left, stats_right, roots_left, roots_right,
        )
    ])
    return pl.pallas_call(
        store_kernel,
        name="store",
        out_shape=[
            jax.ShapeDtypeStruct(params.shape, BF16),
            jax.ShapeDtypeStruct((CAP,) + square, F32),
            jax.ShapeDtypeStruct((CAP,) + square, F32),
        ],
        in_specs=[VMEM] * 2,
        out_specs=[HBM] * 3,
        scratch_shapes=[dma((6,))],
        compiler_params=pltpu.CompilerParams(vmem_limit_bytes=1 << 20),
    )(
        pltpu.with_memory_space_constraint(result, pltpu.VMEM),
        pltpu.with_memory_space_constraint(gram, pltpu.VMEM),
    )


def solution(mesh):
    in_specs = (
        P("dp", None, "fsdp", None),
        P(None, "fsdp", None),
        P(("dp", "fsdp"), None, None),
        P(("dp", "fsdp"), None, None),
        P(("dp", "fsdp"), None, None),
        P(("dp", "fsdp"), None, None),
        P(),
        P(),
    )
    out_specs = (
        P(None, "fsdp", None),
        P(("dp", "fsdp"), None, None),
        P(("dp", "fsdp"), None, None),
    )
    return jax.shard_map(body, mesh=mesh, in_specs=in_specs, out_specs=out_specs, check_vma=False)
```

```python
import jax
import jax.numpy as jnp
from jax import lax
from jax.experimental import pallas as pl
from jax.experimental.pallas import tpu as pltpu
from jax.sharding import PartitionSpec as P

MESH = pl.DeviceIdType.MESH
F32 = jnp.float32
BF16 = jnp.bfloat16

beta_decay = 0.9
learn_rate = 0.2
epsilon = 1e-06
ITERS = 6

PLANES = 4
SIDE = 4
COLS = SIDE * SIDE
CORES = 2
CAP = 2
ROWS = 16
WIDTH = 512
SLOTS = CORES * PLANES * CAP * COLS
HOPS = (1, 3, 2)
CHUNKS = HOPS + (0,)
AHEAD, BEHIND, SECOND = range(3)
PARTS = ((0, 0, COLS // 2, 2), (0, COLS // 2, COLS // 2, 2), (1, 0, COLS, 1))


class Place:
    def __init__(self):
        dp = lax.axis_index("dp")
        fsdp = lax.axis_index("fsdp")
        self.core = lax.rem(dp, 2)
        self.plane = (dp // 2) * 2 + fsdp // COLS
        self.low = fsdp // COLS
        self.col = lax.rem(fsdp, COLS)

    def at(self, core, plane, col):
        return ((plane // 2) * 2 + core, lax.rem(plane, 2) * COLS + col)

    def sibling(self):
        return self.at(1 - self.core, self.plane, self.col)

    def up(self, hop):
        return lax.rem(self.plane + hop, PLANES)

    def above(self, hop):
        return self.at(self.core, self.up(hop), self.col)

    def turn(self, t):
        y, x = self.col // SIDE, lax.rem(self.col, SIDE)
        return lax.rem(y + t // SIDE, SIDE) * SIDE + lax.rem(x + lax.rem(t, SIDE), SIDE)

    def turned(self, t):
        y, x = self.col // SIDE, lax.rem(self.col, SIDE)
        return lax.rem(y + SIDE - t // SIDE, SIDE) * SIDE + lax.rem(x + SIDE - lax.rem(t, SIDE), SIDE)

    def half(self, which):
        return 1 - self.low if which == 0 else self.low


def greet(place):
    partners = [place.sibling()] + [place.above(hop) for hop in HOPS]
    partners += [place.at(place.core, place.plane, place.turn(t)) for t in range(1, COLS)]
    for partner in partners:
        pl.semaphore_signal(pltpu.get_barrier_semaphore(), inc=1, device_id=partner, device_id_type=MESH)
    return len(partners)


def spread_order(i):
    return lax.rem(5 * i, COLS)


def count_up(mask, axis):
    return jnp.sum(mask.astype(jnp.int32), axis=axis, keepdims=True)


def index_tables(owner, refresh, device):
    count = owner.shape[1]
    row = lax.broadcasted_iota(jnp.int32, (count, count), 0)
    column = lax.broadcasted_iota(jnp.int32, (count, count), 1)
    owner_down = jnp.sum(jnp.where(row == column, owner, 0), axis=1, keepdims=True)
    refresh_down = jnp.sum(jnp.where(row == column, refresh, 0), axis=1, keepdims=True)
    same = owner_down == owner
    other_down = count_up(((owner_down ^ 1) == owner) & (refresh > 0), 1)
    ahead_down = (refresh_down > 0) | (((owner_down & 1) == 0) & (other_down == 0))
    rank = count_up(same & (row < column), 0)
    rank_down = count_up(same & (column < row), 1)

    def first(own):
        core, plane = (own >> 5) & 1, 2 * (own >> 6) + ((own >> 4) & 1)
        return (core * PLANES + plane) * CAP * COLS

    entry = first(owner) + (rank + refresh) * COLS + (owner & (COLS - 1))
    col_down = owner_down & (COLS - 1)
    pair_down = (col_down >> 1) + jnp.where(ahead_down, 0, COLS // 2)
    place_down = first(owner_down) + jnp.where(rank_down > 0, COLS + col_down, pair_down)
    spot = lax.broadcasted_iota(jnp.int32, (count, SLOTS), 1)
    block = lax.broadcasted_iota(jnp.int32, (count, SLOTS), 0)
    packed = jnp.sum(jnp.where(place_down == spot, block, 0), axis=0, keepdims=True)
    mine = owner == device
    live = [count_up(mine & (rank == slot), 1) for slot in range(CAP)]
    fresh = count_up(mine & (refresh > 0), 1)
    other = count_up((owner == (device ^ 1)) & (refresh > 0), 1)
    ahead = (fresh > 0) | (((device & 1) == 0) & (other == 0))
    return jnp.minimum(packed, count - 1), jnp.minimum(entry, SLOTS - 1), live, fresh, ahead


def remote(src, dst, send, recv, device):
    return pltpu.make_async_remote_copy(
        src_ref=src, dst_ref=dst, send_sem=send, recv_sem=recv, device_id=device, device_id_type=MESH
    )


def dot(left, right):
    return jnp.dot(left, right, preferred_element_type=F32)


def dot_t(left, right, dims):
    return lax.dot_general(left, right, ((dims, dims), ((), ())), preferred_element_type=F32)


def halves(value):
    high = value.astype(BF16)
    return high, (value - high.astype(F32)).astype(BF16)


def total_square(value):
    return jnp.sum(value * value, axis=(0, 1), keepdims=True)


def root_start(factor, result, mixed, pair):
    scale = jnp.sqrt(total_square(factor) + epsilon)
    start = factor * (1.0 / scale)
    mixed[...] = start
    row = lax.broadcasted_iota(jnp.int32, start.shape, 0)
    column = lax.broadcasted_iota(jnp.int32, start.shape, 1)
    ident = jnp.where(row == column, 1.0, 0.0).astype(F32)
    first = lax.rsqrt(jnp.sqrt(scale)) * (1.25 * ident - 0.25 * start)
    result[...] = first
    pair[0:WIDTH] = start.astype(BF16)
    pair[WIDTH : 2 * WIDTH] = first.astype(BF16)


def root_sweep(results, mixeds, pairs, with_result):
    sides = range(len(results))
    lows = [pair[0:WIDTH] for pair in pairs]
    products = [dot(pairs[i][...] if with_result else lows[i], lows[i]) for i in sides]
    edges = [(products[i][0:WIDTH] - 10.0 * mixeds[i][...]) * (1.0 / 16.0) for i in sides]
    edge_lows = [edge.astype(BF16) for edge in edges]
    fourths = [dot(edge_lows[i], edge_lows[i]) + 3.125 * edges[i] for i in sides]
    if with_result:
        for i in sides:
            value = 1.25 * results[i][...] - 0.25 * products[i][WIDTH : 2 * WIDTH]
            results[i][...] = value
            pairs[i][WIDTH : 2 * WIDTH] = value.astype(BF16)
    for i in sides:
        value = (625.0 / 256.0) * mixeds[i][...] + dot(fourths[i].astype(BF16), lows[i])
        mixeds[i][...] = value
        pairs[i][0:WIDTH] = value.astype(BF16)


def root_end(result, pair):
    return 1.25 * result[...] - 0.25 * dot(pair[WIDTH : 2 * WIDTH], pair[0:WIDTH])


def scaled_step(precond, grad):
    ratio = jnp.sqrt(total_square(grad.astype(F32))) / jnp.sqrt(total_square(precond) + epsilon)
    return (learn_rate * precond * ratio).astype(BF16)


def kept_step(left, grad, right):
    inner = dot(left, grad)
    inner_high, inner_low = halves(inner[0:WIDTH] + inner[WIDTH : 2 * WIDTH])
    right_high, right_low = right[0:WIDTH], right[WIDTH : 2 * WIDTH]
    precond = dot(inner_high, right_high) + (dot(inner_low, right_high) + dot(inner_high, right_low))
    return scaled_step(precond, grad)


def whole_kernel(
    owner_hbm, refresh_hbm, grad_hbm, params_hbm, stats_left, stats_right, roots_left, roots_right,
    result_ref, gram,
    owner_ref, refresh_ref, table_vmem, table, grad_ref, keep, split, inverse, mixed, pair,
    core_out, core_in, plane_out, plane_in, col_out, held, step, rows, every,
    local_sems, core_s, core_r, plane_s, plane_r, col_s, col_r,
    row_s, row_r, up_s, up_r, back_s, back_r, core_s2, core_r2,
):
    place = Place()
    loads = [
        pltpu.make_async_copy(owner_hbm, owner_ref, local_sems.at[7]),
        pltpu.make_async_copy(refresh_hbm, refresh_ref, local_sems.at[8]),
        pltpu.make_async_copy(grad_hbm.at[0], grad_ref, local_sems.at[0]),
    ]
    for copy in loads:
        copy.start()
    partners = greet(place)
    device = lax.axis_index("dp") * lax.axis_size("fsdp") + lax.axis_index("fsdp")
    loads[0].wait()
    loads[1].wait()
    packed, entry, live, fresh, ahead = index_tables(owner_ref[...], refresh_ref[...], device)
    table_vmem[0:1, :] = packed
    table_vmem[1:2, 0 : entry.shape[1]] = entry
    load_table = pltpu.make_async_copy(table_vmem, table, local_sems.at[6])
    load_table.start()
    pl.semaphore_wait(pltpu.get_barrier_semaphore(), partners)
    load_table.wait()
    loads[2].wait()

    def base(core, hop, part):
        slot, at, _, _ = PARTS[part]
        return ((core * PLANES + place.up(hop)) * CAP + slot) * COLS + at

    core_copies = {}
    plane_copies = {}

    def most(ref, send, recv):
        return remote(ref, ref, send, recv, place.sibling())

    def core_sent(part):
        _, at, size, _ = PARTS[part]
        most(core_out.at[:, pl.ds(at, size)], core_s.at[part], core_r.at[part, 0]).wait_send()

    def plane_sent(part):
        slot, at, size, _ = PARTS[part]
        most(plane_out.at[slot, :, pl.ds(at, size)], plane_s.at[part], plane_r.at[part, 0]).wait_send()

    def pack(part):
        slot, at, size, _ = PARTS[part]
        for h, hop in enumerate(CHUNKS):
            start = base(1 - place.core, hop, part)
            if part == SECOND and h == 0:
                core_sent(AHEAD)
                core_sent(BEHIND)

            def one(e, carry, h=h, start=start):
                core_out[h, at + e] = grad_ref[table[0, start + e]]
                return carry

            lax.fori_loop(0, size, one, 0, unroll=4)
            span = pl.ds(at, size)
            core_copies[part, h] = remote(
                core_out.at[h, span], core_in.at[slot, h, span], core_s.at[part], core_r.at[part, h], place.sibling()
            )
            core_copies[part, h].start()

    def add(part):
        slot, at, size, _ = PARTS[part]
        for h, hop in enumerate(CHUNKS):
            core_copies[part, h].wait_recv()
            start = base(place.core, hop, part)

            def one(e, carry, h=h, hop=hop, start=start):
                total = grad_ref[table[0, start + e]] + core_in[slot, h, at + e]
                if hop:
                    plane_out[slot, h, at + e] = total.astype(BF16)
                else:
                    core_in[slot, h, at + e] = total
                return carry

            lax.fori_loop(0, size, one, 0, unroll=4)
            if hop:
                span = pl.ds(at, size)
                plane_copies[part, h] = remote(
                    plane_out.at[slot, h, span], plane_in.at[slot, h, span], plane_s.at[part], plane_r.at[part, h],
                    place.above(hop),
                )
                if part != SECOND:
                    plane_copies[part, h].start()

    def planes_send(part):
        for h in range(len(HOPS)):
            plane_copies[part, h].start()

    def col_copy(part, which, t):
        slot, at, _, share = PARTS[part]
        col, half = place.turn(t), place.half(which)
        return remote(
            col_out.at[slot, half, at + col // share], held.at[part, half, place.col],
            col_s.at[part, which], col_r.at[part, which], place.at(place.core, place.plane, col),
        )

    def col_all(part, which):
        return most(held.at[part, place.half(which), pl.ds(0, COLS - 1)], col_s.at[part, which], col_r.at[part, which])

    def fold(part, which):
        slot, at, size, share = PARTS[part]
        half = place.half(which)
        for h, hop in enumerate(HOPS):
            if (hop == 2) == (which == 1):
                plane_copies[part, h].wait_recv()

        def one(e, carry):
            if which == 0:
                total = plane_in[slot, 0, at + e].astype(F32) + plane_in[slot, 1, at + e].astype(F32)
            else:
                total = core_in[slot, len(HOPS), at + e] + plane_in[slot, 2, at + e].astype(F32)
            col_out[slot, half, at + e] = total.astype(BF16)
            return carry

        lax.fori_loop(0, size, one, 0, unroll=4)

        def send(i, carry):
            col_copy(part, which, spread_order(i)).start()
            return carry

        lax.fori_loop(1, COLS, send, 0)
        held[part, half, place.col] = col_out[slot, half, at + place.col // share]

    def col_wait(part):
        for which in range(2):
            col_all(part, which).wait_recv()

    def region(plane, slot):
        return ((place.core * PLANES + plane) * CAP + slot) * COLS

    def row_copy(slot, t):
        col = place.turn(t)
        return remote(
            step.at[slot, 1 - place.low, col], rows.at[slot, place.col],
            row_s.at[slot], row_r.at[slot, t], place.at(place.core, place.plane, col),
        )

    def back_copy(slot, far, t):
        plane, col = place.up(2 * far), place.turn(t)
        return remote(
            step.at[slot, place.low, col], every.at[region(place.plane, slot) + place.col],
            back_s.at[slot], back_r.at[slot, far], place.at(place.core, plane, col),
        )

    def up_copy(slot, h, t):
        col = place.turned(t)
        return remote(
            rows.at[slot, col], every.at[region(place.plane, slot) + col],
            up_s.at[slot], up_r.at[slot, h], place.above(HOPS[h]),
        )

    def rows_send(slot):
        def one(i, carry):
            row_copy(slot, spread_order(i)).start()
            return carry

        lax.fori_loop(1, COLS, one, 0)
        rows[slot, place.col] = step[slot, 1 - place.low, place.col]

    def back_send(slot, to_far=True, to_here=True):
        def far(i, carry):
            back_copy(slot, 1, spread_order(i)).start()
            return carry

        def here(i, carry):
            back_copy(slot, 0, spread_order(i)).start()
            return carry

        if to_far:
            lax.fori_loop(0, COLS, far, 0)
        if not to_here:
            return
        lax.fori_loop(1, COLS, here, 0)
        every[region(place.plane, slot) + place.col] = step[slot, place.low, place.col]

    def back_up(slot):
        def up(t):
            for h in range(2):
                up_copy(slot, h, t).start()

        def one(i, carry):
            row_copy(slot, spread_order(i)).wait_recv()
            up(spread_order(i))
            return carry

        up(0)
        lax.fori_loop(1, COLS, one, 0)

    def piece(count):
        return every.at[pl.ds(0, count)]

    def row_all(slot):
        return most(rows.at[slot, pl.ds(0, COLS - 1)], row_s.at[slot], row_r.at[slot, 0])

    def back_all(slot, far):
        return most(piece(COLS - 1 + far), back_s.at[slot], back_r.at[slot, far])

    def up_all(slot, h):
        return most(piece(COLS), up_s.at[slot], up_r.at[slot, h])

    def back_over(slot):
        for h in (3, 2, 0, 1):
            if h < 2:
                up_all(slot, h).wait_recv()
            else:
                back_all(slot, 3 - h).wait_recv()
            over(slot, h)

    def back_sent(slot):
        row_all(slot).wait_send()
        most(piece(2 * COLS - 1), back_s.at[slot], back_r.at[slot, 0]).wait_send()
        most(piece(2 * COLS), up_s.at[slot], up_r.at[slot, 0]).wait_send()

    core_all = most(piece(SLOTS // 2), core_s2.at[0], core_r2.at[0])

    def over(slot, h):
        here = every.at[pl.ds(region(place.up(PLANES - CHUNKS[h]), slot), COLS)]
        remote(here, here, core_s2.at[0], core_r2.at[0], place.sibling()).start()

    pack(AHEAD)
    pack(BEHIND)
    add(AHEAD)
    loads = []
    for i, (src, dst) in enumerate(
        ((roots_left, keep.at[0]), (roots_right, keep.at[1]), (stats_left, gram.at[0]), (stats_right, gram.at[1]),
         (params_hbm, result_ref))
    ):
        copy = pltpu.make_async_copy(src, dst, local_sems.at[1 + i])
        copy.start()
        loads.append(copy)
    add(BEHIND)
    pack(SECOND)
    for copy in loads[:2]:
        copy.wait()
    for side in range(2):
        for slot in range(CAP):
            high, low = halves(keep[side, slot])
            split[side, slot, 0:WIDTH] = high
            split[side, slot, WIDTH : 2 * WIDTH] = low
    fold(AHEAD, 0)
    fold(AHEAD, 1)
    add(SECOND)
    fold(BEHIND, 0)
    planes_send(SECOND)
    fold(BEHIND, 1)
    for copy in loads[2:]:
        copy.wait()

    def grad_of(part):
        return held[part].reshape(WIDTH, WIDTH)

    def first_grad():
        both = jnp.where(ahead, grad_of(AHEAD).astype(F32), grad_of(BEHIND).astype(F32))
        return both.astype(BF16)

    def put_step(slot, value):
        step[slot] = value.reshape(2, COLS, ROWS, WIDTH)

    def factor(side, slot, grad):
        fresh_part = dot_t(grad, grad, ((1,), (0,))[side])
        return beta_decay * gram[side, slot] + ((1.0 - beta_decay) / WIDTH) * fresh_part

    def factors(slot, grad):
        for side in range(2):
            gram[side, slot] = live[slot].astype(F32) * factor(side, slot, grad)

    def sweep(with_result):
        root_sweep(
            [inverse.at[0], inverse.at[1]], [mixed.at[0], mixed.at[1]], [pair.at[0], pair.at[1]], with_result
        )

    def sweeps(count):
        def one(i, carry):
            sweep(True)
            return carry

        lax.fori_loop(0, count, one, 0)

    col_wait(AHEAD)
    for side in range(2):
        root_start(factor(side, 0, grad_of(AHEAD)), inverse.at[side], mixed.at[side], pair.at[side])
    sweep(False)
    sweep(True)
    col_wait(BEHIND)
    put_step(0, kept_step(split[0, 0], first_grad(), split[1, 0]))
    rows_send(0)
    fold(SECOND, 0)
    fold(SECOND, 1)
    back_send(0)
    sweeps(1)
    back_up(0)
    sweeps(2)
    col_wait(SECOND)
    put_step(1, kept_step(split[0, 1], grad_of(SECOND), split[1, 1]))
    grad = grad_of(AHEAD)
    root_left, root_right = [root_end(inverse.at[side], pair.at[side]).astype(BF16) for side in range(2)]
    renewed = scaled_step(dot(dot(root_left, grad).astype(BF16), root_right), grad)
    late = step[1].reshape(WIDTH, WIDTH)
    put_step(1, jnp.where(fresh > 0, renewed.astype(F32), late.astype(F32)).astype(BF16))
    rows_send(1)
    back_send(1, to_here=False)
    back_up(1)
    back_send(1, to_far=False)
    back_over(0)
    factors(0, first_grad())
    factors(1, grad_of(SECOND))
    core_sent(SECOND)
    for part in range(len(PARTS)):
        plane_sent(part)
    for part in range(len(PARTS)):
        for which in range(2):
            col_all(part, which).wait_send()
    back_sent(0)
    back_over(1)
    back_sent(1)
    core_all.wait_recv()

    def apply(b, carry):
        change = every[table[1, b]].astype(F32)
        result_ref[b] = (result_ref[b].astype(F32) - change).astype(BF16)
        return carry

    lax.fori_loop(0, result_ref.shape[0], apply, 0, unroll=4)
    core_all.wait_send()


def store_kernel(result_ref, gram, out_params, out_left, out_right, sems):
    copies = []
    for slot in range(CAP):
        copies.append((gram.at[0, slot], out_left.at[slot]))
        copies.append((gram.at[1, slot], out_right.at[slot]))
    half = result_ref.shape[0] // 2
    for part in range(2):
        span = pl.ds(part * half, half)
        copies.append((result_ref.at[span], out_params.at[span]))
    copies = [pltpu.make_async_copy(src, dst, sems.at[i]) for i, (src, dst) in enumerate(copies)]
    for copy in copies:
        copy.start()
    for copy in copies:
        copy.wait()


VMEM = pl.BlockSpec(memory_space=pltpu.VMEM)
HBM = pl.BlockSpec(memory_space=pltpu.HBM)


def body(grad_partial, params, stats_left, stats_right, roots_left, roots_right, owner, refresh):
    count = params.shape[0]
    dma = pltpu.SemaphoreType.DMA
    hops = len(HOPS)
    piece = (COLS, ROWS, WIDTH)
    square = (WIDTH, WIDTH)
    result, gram = pl.pallas_call(
        whole_kernel,
        name="whole",
        out_shape=[pltpu.VMEM(params.shape, BF16), pltpu.VMEM((2, CAP) + square, F32)],
        in_specs=[HBM] * 8,
        out_specs=[VMEM] * 2,
        scratch_shapes=[
            pltpu.VMEM((1, count), jnp.int32),
            pltpu.VMEM((1, count), jnp.int32),
            pltpu.VMEM((8, SLOTS), jnp.int32),
            pltpu.SMEM((8, SLOTS), jnp.int32),
            pltpu.VMEM((count, ROWS, WIDTH), F32),
            pltpu.VMEM((2, CAP) + square, F32),
            pltpu.VMEM((2, CAP, 2 * WIDTH, WIDTH), BF16),
            pltpu.VMEM((2,) + square, F32),
            pltpu.VMEM((2,) + square, F32),
            pltpu.VMEM((2, 2 * WIDTH, WIDTH), BF16),
            pltpu.VMEM((PLANES,) + piece, F32),
            pltpu.VMEM((CAP, PLANES) + piece, F32),
            pltpu.VMEM((CAP, hops) + piece, BF16),
            pltpu.VMEM((CAP, hops) + piece, BF16),
            pltpu.VMEM((CAP, 2) + piece, BF16),
            pltpu.VMEM((len(PARTS), 2) + piece, BF16),
            pltpu.VMEM((CAP, 2) + piece, BF16),
            pltpu.VMEM((CAP,) + piece, BF16),
            pltpu.VMEM((SLOTS, ROWS, WIDTH), BF16),
            dma((9,)),
            dma((len(PARTS),)), dma((len(PARTS), PLANES)),
            dma((len(PARTS),)), dma((len(PARTS), hops)),
            dma((len(PARTS), 2)), dma((len(PARTS), 2)),
            dma((CAP,)), dma((CAP, COLS)),
            dma((CAP,)), dma((CAP, 2)),
            dma((CAP,)), dma((CAP, 2)),
            dma((1,)), dma((1,)),
        ],
        compiler_params=pltpu.CompilerParams(collective_id=0, has_side_effects=True, vmem_limit_bytes=46 << 20),
    )(*[
        pltpu.with_memory_space_constraint(array, pltpu.HBM)
        for array in (
            owner.reshape(1, count), refresh.reshape(1, count),
            grad_partial, params, stats_left, stats_right, roots_left, roots_right,
        )
    ])
    return pl.pallas_call(
        store_kernel,
        name="store",
        out_shape=[
            jax.ShapeDtypeStruct(params.shape, BF16),
            jax.ShapeDtypeStruct((CAP,) + square, F32),
            jax.ShapeDtypeStruct((CAP,) + square, F32),
        ],
        in_specs=[VMEM] * 2,
        out_specs=[HBM] * 3,
        scratch_shapes=[dma((6,))],
        compiler_params=pltpu.CompilerParams(vmem_limit_bytes=1 << 20),
    )(
        pltpu.with_memory_space_constraint(result, pltpu.VMEM),
        pltpu.with_memory_space_constraint(gram, pltpu.VMEM),
    )


def solution(mesh):
    in_specs = (
        P("dp", None, "fsdp", None),
        P(None, "fsdp", None),
        P(("dp", "fsdp"), None, None),
        P(("dp", "fsdp"), None, None),
        P(("dp", "fsdp"), None, None),
        P(("dp", "fsdp"), None, None),
        P(),
        P(),
    )
    out_specs = (
        P(None, "fsdp", None),
        P(("dp", "fsdp"), None, None),
        P(("dp", "fsdp"), None, None),
    )
    return jax.shard_map(body, mesh=mesh, in_specs=in_specs, out_specs=out_specs, check_vma=False)
```
